32 devices in a mesh: seq: 16 (over z, y, x), tp: 2 (over core).
Axes of the slice: x: 2, y: 2, z: 4, core: 2. Of those that a mesh axis runs over, the one named last changes fastest.
Arguments:
- tokens: bfloat16 [4096, 4096], P('seq', 'tp'), may hold values from -6 to 6
- x_weight: bfloat16 [4096, 2048], P('seq', 'tp'), may hold values from -0.09375 to 0.09375
- bc_weight: bfloat16 [4096, 256], P('seq', 'tp'), may hold values from -0.09375 to 0.09375
- dt_weight: bfloat16 [4096, 32], P('seq', 'tp'), may hold values from -0.09375 to 0.09375
- conv_x: float32 [4, 2048], P(None, 'tp'), may hold values from -2.5 to 2.5
- conv_bc: float32 [4, 256], replicated, may hold values from -2.5 to 2.5
- dt_bias: float32 [32], P('tp'), may hold values from -3 to 0
- decay_rate: float32 [32], P('tp'), may hold values from 2.4414062e-06 to 0.07
- d_skip: float32 [32], P('tp'), may hold values from 0.5 to 2
- norm_gain: float32 [2048], P('tp'), may hold values from 0.5 to 1.5
- initial_state: float32 [32, 64, 128], P('tp'), may hold values from -16 to 16
- steer: float32 [2048], P('tp'), may hold values from -6 to 6
Outputs:
- steered: bfloat16 [4096, 2048], P('seq', 'tp')
The draws below stay inside these ranges and needn't reach their ends.
All inputs are finite; a program needn't handle non-finite values.
Results may differ from the reference program's by a relative error of at most 0.0055.
Values may be sent and summed in bfloat16 or wider, within the bound.
A program may use at most 64 MiB of HBM per device.

```python
import math
import jax
import jax.numpy as jnp
from jax import lax

D = 4096
P_SIZE = 64
N = 128
WIDTH = 4
GROUP = 128
HEADS = 32
INNER = 2048
TOKENS = 4096


def shard_levels(own_key, shape, pieces, low, largest):
    gain, own = 1.0, jax.random.fold_in(own_key, 6)
    for axis_at, blocks in pieces:
        draws = jnp.exp(jax.random.uniform(jax.random.fold_in(own, axis_at), (blocks,), jnp.float32, low / len(pieces), largest / len(pieces)))
        gain = gain * jnp.repeat(draws, shape[axis_at] // blocks).reshape([-1 if axis == axis_at else 1 for axis in range(len(shape))])
    return gain


def noise(rng, dims, width, bound, shards=(), kind=jnp.bfloat16):
    drawn = jax.random.normal(rng, dims, jnp.float32) * width
    if len(shards) > 0:
        drawn = shard_levels(rng, dims, shards, -0.22, 0.18) * drawn
    return jnp.clip(drawn, min=-bound, max=bound).astype(kind)


def setup_inputs(seed: int = 0) -> dict:
    splits = jax.random.split(jax.random.key(seed), 13)
    tokens = noise(splits[0], (TOKENS, D), 1.0, 6.0, ((0, 16), (1, 2)))
    x_weight = noise(splits[1], (D, INNER), D ** -0.5, 0.09375, ((0, 16), (1, 2)))
    bc_weight = noise(splits[2], (D, 2 * N), D ** -0.5, 0.09375, ((0, 16), (1, 2)))
    dt_weight = noise(splits[3], (D, HEADS), D ** -0.5, 0.09375, ((0, 16), (1, 2)))
    conv_x = noise(splits[4], (WIDTH, INNER), 0.5, 2.5, ((1, 2),), jnp.float32)
    conv_bc = noise(splits[5], (WIDTH, 2 * N), 0.5, 2.5, (), jnp.float32)
    dt_bias = jnp.clip(-3.0 + 3.0 * jax.random.uniform(splits[6], (HEADS,), jnp.float32) ** shard_levels(splits[6], (HEADS,), ((0, 2),), -0.2, 0.2), -3.0, 0.0)
    decay_rate = jnp.clip(jnp.exp(math.log(0.07) - 10.2636763 * jax.random.uniform(splits[7], (HEADS,), jnp.float32) ** shard_levels(splits[7], (HEADS,), ((0, 2),), -0.2, 0.2)), 2.441406195430318e-06, 0.07)
    d_skip = jnp.clip(jnp.exp(math.log(2.0) - 1.3862944 * jax.random.uniform(splits[8], (HEADS,), jnp.float32) ** shard_levels(splits[8], (HEADS,), ((0, 2),), -0.2, 0.2)), 0.5, 2.0)
    norm_gain = jnp.clip(1.0 + 0.1 * jax.random.normal(splits[9], (INNER,), jnp.float32), 0.5, 1.5)
    initial_state = noise(splits[10], (HEADS, P_SIZE, N), 4.0, 16.0, ((0, 2),), jnp.float32)
    steer = noise(splits[11], (INNER,), 1.0, 6.0, ((0, 2),), jnp.float32)
    return dict(tokens=tokens, x_weight=x_weight, bc_weight=bc_weight, dt_weight=dt_weight, conv_x=conv_x, conv_bc=conv_bc, dt_bias=dt_bias, decay_rate=decay_rate, d_skip=d_skip, norm_gain=norm_gain, initial_state=initial_state, steer=steer)


EPSILON = 1e-05

def convolve(pre_values, kernel):
    kernel_rows = kernel.shape[0]
    length = pre_values.shape[0]
    padded = jnp.concatenate([jnp.zeros((kernel_rows - 1, pre_values.shape[1]), pre_values.dtype), pre_values], 0)
    summed = kernel[0] * padded[0:length].astype(jnp.float32)
    for offset in range(1, kernel_rows):
        summed = summed + kernel[offset] * padded[offset:offset + length].astype(jnp.float32)
    return jax.nn.silu(summed).astype(jnp.bfloat16)

def reference(tokens, x_weight, bc_weight, dt_weight, conv_x, conv_bc, dt_bias, decay_rate, d_skip, norm_gain, initial_state, steer):
    x_pre = jnp.dot(tokens, x_weight, preferred_element_type=jnp.float32).astype(jnp.bfloat16)
    bc_pre = jnp.dot(tokens, bc_weight, preferred_element_type=jnp.float32).astype(jnp.bfloat16)
    dt_raw = jnp.dot(tokens, dt_weight, preferred_element_type=jnp.float32)
    x_conv = convolve(x_pre, conv_x)
    bc_conv = convolve(bc_pre, conv_bc)
    step_size = jax.nn.softplus(dt_raw + dt_bias[None, :])
    log_decay = -step_size * decay_rate[None, :]
    blocks = TOKENS // GROUP
    x_blocks = x_conv.reshape(blocks, GROUP, HEADS, P_SIZE)
    b_blocks = bc_conv[:, :N].reshape(blocks, GROUP, N)
    c_blocks = bc_conv[:, N:].reshape(blocks, GROUP, N)
    a_blocks = log_decay.reshape(blocks, GROUP, HEADS)
    dt_blocks = step_size.reshape(blocks, GROUP, HEADS)
    steer_rows = steer.reshape(HEADS, P_SIZE)
    gain_rows = norm_gain.reshape(HEADS, P_SIZE)
    causal = lax.broadcasted_iota(jnp.int32, (GROUP, GROUP), 0) >= lax.broadcasted_iota(jnp.int32, (GROUP, GROUP), 1)

    def block_update(carry_state, inputs):
        x_block, b_block, c_block, a_block, dt_block = inputs
        cumulative = jnp.cumsum(a_block, axis=0)
        scores = jnp.dot(c_block, b_block.T, preferred_element_type=jnp.float32)
        differ = cumulative[:, None, :] - cumulative[None, :, :]
        decays = jnp.where(causal[:, :, None], jnp.exp(jnp.where(causal[:, :, None], differ, 0.0)), 0.0)
        mixing = (scores[:, :, None] * decays * dt_block[None, :, :]).astype(jnp.bfloat16)
        x_float = x_block.astype(jnp.float32)
        inside = jnp.einsum('tsh,shp->thp', mixing.astype(jnp.float32), x_float)
        carried_in = jnp.einsum('tn,hpn->thp', c_block.astype(jnp.float32), carry_state, precision=lax.Precision.HIGHEST)
        outputs = inside + jnp.exp(cumulative)[:, :, None] * carried_in + d_skip[None, :, None] * x_float
        to_end = jnp.exp(cumulative[-1][None, :] - cumulative) * dt_block
        scaled = (x_float * to_end[:, :, None]).astype(jnp.bfloat16)
        added_state = jnp.einsum('shp,sn->hpn', scaled.astype(jnp.float32), b_block.astype(jnp.float32))
        next_state = jnp.exp(cumulative[-1])[:, None, None] * carry_state + added_state
        mean_square = lax.optimization_barrier(jnp.mean(outputs * outputs, axis=-1, keepdims=True))
        normed = outputs * lax.rsqrt(mean_square + EPSILON) * gain_rows[None, :, :]
        penalty = lax.optimization_barrier(jnp.sum(normed * steer_rows[None, :, :], axis=(1, 2))) / jnp.sqrt(jnp.float32(INNER))
        result = (normed - penalty[:, None, None] * steer_rows[None, :, :]).astype(jnp.bfloat16)
        return (next_state, result)
    final_state, results = lax.scan(block_update, initial_state.astype(jnp.float32), (x_blocks, b_blocks, c_blocks, a_blocks, dt_blocks))
    return results.reshape(TOKENS, INNER)
```

```python
import functools

import jax
import jax.numpy as jnp
from jax import lax
from jax.experimental import pallas as pl
from jax.experimental.pallas import tpu as pltpu
from jax.sharding import PartitionSpec as P

MESH = pl.DeviceIdType.MESH
PLANE = 4
TAIL = 16
F32 = jnp.float32
BF16 = jnp.bfloat16

N = 128
GROUP = 128


EPSILON = 1e-05


def passed_along(value, axis, steps):
    count = lax.axis_size(axis)
    first, last = (max(0, -steps), min(count, count - steps))
    return lax.ppermute(value, axis, [(source, source + steps) for source in range(first, last)])


def prefix(x, axis, combine, identity):
    count, mine = (lax.axis_size(axis), lax.axis_index(axis))
    everything = jax.tree.map(
        lambda part, kind: lax.all_gather(part.astype(kind), axis), x, (jnp.bfloat16, jnp.bfloat16)
    )
    start = jax.tree.map(
        lambda part, zero: jnp.broadcast_to(jnp.asarray(zero, part.dtype), part.shape), x, identity
    )

    def turn(k, before):
        reached = k < mine
        new = combine(
            before, jax.tree.map(lambda part, own: part[k].astype(own.dtype), everything, x)
        )
        return jax.tree.map(lambda a, b: jnp.where(reached, a, b), new, before)

    return lax.fori_loop(0, count, turn, start)


def convolve(extended, kernel):
    kernel_rows = kernel.shape[0]
    length = extended.shape[0] - kernel_rows + 1
    summed = kernel[0] * extended[0:length].astype(jnp.float32)
    for offset in range(1, kernel_rows):
        summed = summed + kernel[offset] * extended[offset : offset + length].astype(jnp.float32)
    return jax.nn.silu(summed).astype(jnp.bfloat16)


def block_update(carry_state, inputs):
    x_block, b_block, c_block, a_block, dt_block = inputs
    length = a_block.shape[0]
    cumulative = jnp.cumsum(a_block, axis=0)
    scores = jnp.dot(c_block, b_block.T, preferred_element_type=jnp.float32)
    causal = lax.broadcasted_iota(jnp.int32, (length, length), 0) >= lax.broadcasted_iota(
        jnp.int32, (length, length), 1
    )
    differ = cumulative[:, None, :] - cumulative[None, :, :]
    decays = jnp.where(causal[:, :, None], jnp.exp(jnp.where(causal[:, :, None], differ, 0.0)), 0.0)
    mixing = (scores[:, :, None] * decays * dt_block[None, :, :]).astype(jnp.bfloat16)
    inside = jnp.einsum("tsh,shp->thp", mixing, x_block, preferred_element_type=jnp.float32)
    carried_in = jnp.einsum(
        "tn,hpn->thp", c_block.astype(jnp.float32), carry_state, precision=lax.Precision.HIGHEST
    )
    outputs = inside + jnp.exp(cumulative)[:, :, None] * carried_in
    to_end = jnp.exp(cumulative[-1][None, :] - cumulative) * dt_block
    scaled = (x_block.astype(jnp.float32) * to_end[:, :, None]).astype(jnp.bfloat16)
    added_state = jnp.einsum("shp,sn->hpn", scaled, b_block, preferred_element_type=jnp.float32)
    return (jnp.exp(cumulative[-1])[:, None, None] * carry_state + added_state, outputs)


def combine_carry(earlier, later):
    return (earlier[0] * later[0], later[0][:, None, None] * earlier[1] + later[1])


def portable(
    tokens,
    x_weight,
    bc_weight,
    dt_weight,
    conv_x,
    conv_bc,
    dt_bias,
    decay_rate,
    d_skip,
    norm_gain,
    initial_state,
    steer,
):
    features = lax.all_gather(tokens, "tp", axis=1, tiled=True)
    rim_rows = conv_x.shape[0] - 1
    local_tokens = features.shape[0]
    head_count = dt_weight.shape[1]
    channels = x_weight.shape[1]
    head_size = channels // head_count
    bc_panel = lax.all_gather(bc_weight, "tp", axis=1, tiled=True)
    previous = passed_along(features[local_tokens - rim_rows :], "seq", 1)
    source = jnp.concatenate([previous, features], 0)
    x_sums = jnp.dot(
        source,
        lax.all_gather(x_weight, "seq", axis=0, tiled=True),
        preferred_element_type=jnp.float32,
    )
    bc_sums = jnp.dot(
        source,
        lax.all_gather(bc_panel, "seq", axis=0, tiled=True),
        preferred_element_type=jnp.float32,
    )
    dt_sums = jnp.dot(
        source,
        lax.all_gather(dt_weight, "seq", axis=0, tiled=True),
        preferred_element_type=jnp.float32,
    )
    x_pre = x_sums.astype(jnp.bfloat16)
    bc_pre = bc_sums.astype(jnp.bfloat16)
    dt_raw = dt_sums[rim_rows:]
    x_conv = convolve(x_pre, conv_x)
    bc_conv = convolve(bc_pre, conv_bc)
    b_values = bc_conv[:, :N]
    c_values = bc_conv[:, N:]
    step_size = jax.nn.softplus(dt_raw + dt_bias[None, :])
    log_decay = -step_size * decay_rate[None, :]
    blocks = local_tokens // GROUP
    x_heads = x_conv.reshape(local_tokens, head_count, head_size)
    inputs = (
        x_heads.reshape(blocks, GROUP, head_count, head_size),
        b_values.reshape(blocks, GROUP, N),
        c_values.reshape(blocks, GROUP, N),
        log_decay.reshape(blocks, GROUP, head_count),
        step_size.reshape(blocks, GROUP, head_count),
    )
    zero_state = jnp.zeros((head_count, head_size, N), jnp.float32)
    local_state, local_out = lax.scan(block_update, zero_state, inputs)
    running = jnp.cumsum(log_decay, axis=0)
    local_decay = jnp.exp(running[-1])
    identity = (
        jnp.ones((head_count,), jnp.float32),
        jnp.zeros((head_count, head_size, N), jnp.float32),
    )
    prefix_decay, prefix_state = prefix((local_decay, local_state), "seq", combine_carry, identity)
    entering = prefix_decay[:, None, None] * initial_state + prefix_state
    from_entering = jnp.einsum(
        "tn,hpn->thp", c_values.astype(jnp.float32), entering, precision=lax.Precision.HIGHEST
    )
    outputs = (
        local_out.reshape(local_tokens, head_count, head_size)
        + jnp.exp(running)[:, :, None] * from_entering
        + d_skip[None, :, None] * x_heads.astype(jnp.float32)
    )
    mean_square = jnp.mean(outputs * outputs, axis=-1, keepdims=True)
    normed = (outputs * lax.rsqrt(mean_square + EPSILON)).reshape(
        local_tokens, channels
    ) * norm_gain[None, :]
    partial_dot = jnp.sum(normed * steer[None, :], axis=1)
    total_dot = lax.psum(partial_dot, "tp")
    penalty = total_dot / jnp.sqrt(jnp.float32(channels * lax.axis_size("tp")))
    return (normed - penalty[:, None] * steer[None, :]).astype(jnp.bfloat16)


def dot(a, b):
    return jnp.dot(a, b, preferred_element_type=F32)


def split_dot(a, b):
    high = b.astype(BF16)
    low = (b - high.astype(F32)).astype(BF16)
    return dot(a, high) + dot(a, low)


def gather_kernel(
    planes, tok_ref, pack_ref, x_out, bc_out, dt_out, xt_out, bct_out,
    toks, weights, x_keep, bc_keep, x_tail, bc_tail, send_sem, tok_sem, sib_sem, swap_sem, line_sem, tail_sem, own_sem,
):
    seq, core = lax.axis_index("seq"), lax.axis_index("tp")
    plane, member = lax.div(seq, PLANE), lax.rem(seq, PLANE)
    base = plane * PLANE
    own_rows, columns = tok_ref.shape
    half = own_rows // 2
    depth = pack_ref.shape[1] - TAIL
    my_x, my_y = lax.rem(member, 2), lax.div(member, 2)
    members = [member, my_y * 2 + 1 - my_x, (1 - my_y) * 2 + my_x, (1 - my_y) * 2 + 1 - my_x]
    has_below, has_above = plane > 0, plane < planes - 1

    barrier = pltpu.get_barrier_semaphore()

    def greet(s, c):
        pl.semaphore_signal(barrier, inc=1, device_id=(s, c), device_id_type=MESH)

    for j in (1, 2, 3):
        greet(base + members[j], core)
    greet(seq, 1 - core)

    @pl.when(has_below)
    def _():
        greet(seq - PLANE, core)
        greet(seq - PLANE, 1 - core)

    @pl.when(has_above)
    def _():
        greet(seq + PLANE, core)
        greet(seq + PLANE, 1 - core)

    below, above = jnp.where(has_below, 2, 0), jnp.where(has_above, 2, 0)
    pl.semaphore_wait(barrier, 4 + below + above)

    started = []

    def send(source, target, sem, device, when=None):
        copy = pltpu.make_async_remote_copy(
            src_ref=source, dst_ref=target, send_sem=send_sem.at[len(started)], recv_sem=sem,
            device_id=device, device_id_type=MESH,
        )
        started.append((copy, when))
        if when is None:
            copy.start()
        else:
            pl.when(when)(lambda: copy.start())

    def arrived(target, sem, when=None):
        copy = pltpu.make_async_remote_copy(
            src_ref=target, dst_ref=target, send_sem=send_sem.at[0], recv_sem=sem,
            device_id=(seq, 1 - core), device_id_type=MESH,
        )
        if when is None:
            copy.wait_recv()
        else:
            pl.when(when)(lambda: copy.wait_recv())

    def piece(c, j, h):
        return toks.at[c, pl.ds(pl.multiple_of(members[j] * own_rows + h * half, half), half)]

    def own_piece(h):
        return tok_ref.at[pl.ds(h * half, half)]

    def block(p, j):
        return weights.at[p, members[j]]

    across = [(base + members[j], core) for j in range(4)]
    up, down, sibling = (seq + PLANE, core), (seq - PLANE, core), (seq, 1 - core)

    own_weights = pltpu.make_async_copy(pack_ref.at[member], block(plane, 0), own_sem.at[0])
    own_tokens = pltpu.make_async_copy(tok_ref, toks.at[core, pl.ds(pl.multiple_of(member * own_rows, own_rows), own_rows)], own_sem.at[1])
    own_weights.start()
    own_tokens.start()
    for j in (1, 2, 3):
        send(pack_ref.at[members[j]], weights.at[plane, member], swap_sem.at[j], across[j])
    send(pack_ref.at[member], block(plane, 0), line_sem.at[0, 1, 0], up, has_above)
    send(pack_ref.at[member], block(plane, 0), line_sem.at[1, 1, 0], down, has_below)
    send(own_piece(0), piece(core, 0, 0), tok_sem.at[0], across[1])
    send(own_piece(1), piece(core, 0, 1), tok_sem.at[2], across[2])
    send(own_piece(1), piece(core, 0, 1), tok_sem.at[1], across[1])
    send(own_piece(0), piece(core, 0, 0), tok_sem.at[3], across[2])
    send(own_piece(0), piece(core, 0, 0), sib_sem.at[0, 0], sibling)
    send(own_piece(1), piece(core, 0, 1), sib_sem.at[0, 1], sibling)
    for j in (1, 2, 3):
        arrived(block(plane, j), swap_sem.at[j])
        send(block(plane, j), block(plane, j), line_sem.at[0, 1, j], up, has_above)
        send(block(plane, j), block(plane, j), line_sem.at[1, 1, j], down, has_below)

    def relay(step, j):
        lower, upper = plane - step, plane + step
        arrived(block(jnp.maximum(lower, 0), j), line_sem.at[0, step, j], lower >= 0)
        arrived(block(jnp.minimum(upper, planes - 1), j), line_sem.at[1, step, j], upper < planes)
        if step < planes - 1:
            low = block(jnp.maximum(lower, 0), j)
            high = block(jnp.minimum(upper, planes - 1), j)
            send(low, low, line_sem.at[0, step + 1, j], up, jnp.logical_and(lower >= 0, has_above))
            send(high, high, line_sem.at[1, step + 1, j], down, jnp.logical_and(upper < planes, has_below))

    def token(j, h, index, forward=None):
        here = piece(core, j, h)
        arrived(here, tok_sem.at[index])
        if forward is not None:
            send(here, here, tok_sem.at[forward[0]], across[forward[1]])
        send(here, here, sib_sem.at[j, h], sibling)

    steps = [(step, j) for step in range(1, planes) for j in range(4)]
    takes = [
        (1, 0, 0, (4, 2)), (2, 1, 2, (5, 1)), (1, 1, 1, None), (2, 0, 3, None), (3, 0, 4, None), (3, 1, 5, None),
    ]
    places = [3, 3, 7, 7, 11, 11]
    for at, (step, j) in enumerate(steps):
        for take, place in zip(takes, places):
            if place == at:
                token(*take)
        relay(step, j)
    for take, place in zip(takes, places):
        if place >= len(steps):
            token(*take)
    own_weights.wait()
    own_tokens.wait()
    for j in range(4):
        for h in range(2):
            arrived(piece(1 - core, j, h), sib_sem.at[j, h])

    rows = toks.shape[1]
    tile = rows // 2
    channels = x_out.shape[1]
    per_half = columns // depth
    filler = jnp.zeros((128 - TAIL, depth), BF16)

    def multiply(at, _):
        where = pl.ds(pl.multiple_of(at * tile, tile), tile)
        wide = jnp.zeros((tile, channels + 128), F32)
        narrow = jnp.zeros((tile, 128), F32)
        for k in range(2 * per_half):
            left = toks[k // per_half, where, (k % per_half) * depth : (k % per_half + 1) * depth]
            wide += dot(left, weights[k // PLANE, k % PLANE, :depth, :])
            steps_w = jnp.concatenate([weights[k // PLANE, k % PLANE, depth:, :depth], filler], 0)
            narrow += lax.dot_general(left, steps_w, (((1,), (1,)), ((), ())), preferred_element_type=F32)
        x_keep[where, :] = wide[:, :channels].astype(BF16)
        bc_keep[core, where, :] = wide[:, channels:].astype(BF16)
        dt_out[where, :] = narrow
        return 0

    lax.fori_loop(0, 2, multiply, 0)
    last = pl.ds(rows - TAIL, TAIL)
    send(x_keep.at[last], x_tail, tail_sem.at[0], up, has_above)
    send(bc_keep.at[core, last], bc_tail.at[core], tail_sem.at[1], up, has_above)
    send(bc_keep.at[core, last], bc_tail.at[core], tail_sem.at[2], (seq + PLANE, 1 - core), has_above)
    send(bc_keep.at[core], bc_keep.at[core], tail_sem.at[3], sibling)
    x_out[...] = x_keep[...]

    @pl.when(jnp.logical_not(has_below))
    def _():
        x_tail[...] = jnp.zeros_like(x_tail)
        bc_tail[...] = jnp.zeros_like(bc_tail)

    arrived(x_tail, tail_sem.at[0], has_below)
    arrived(bc_tail.at[core], tail_sem.at[1], has_below)
    arrived(bc_tail.at[1 - core], tail_sem.at[2], has_below)
    arrived(bc_keep.at[1 - core], tail_sem.at[3])
    xt_out[...] = x_tail[...]
    bct_out[...] = bc_tail[...]
    bc_out[...] = bc_keep[...]
    for copy, when in started:
        if when is None:
            copy.wait_send()
        else:
            pl.when(when)(lambda copy=copy: copy.wait_send())


def smooth(ref, at, taps):
    rows = ref[pl.ds(pl.multiple_of(at * GROUP + TAIL - 8, 8), GROUP + 8), :]
    width = taps.shape[0]
    summed = taps[0:1, :] * rows[9 - width : 9 - width + GROUP]
    for k in range(1, width):
        summed = summed + taps[k : k + 1, :] * rows[9 - width + k : 9 - width + k + GROUP]
    return (summed / (1.0 + jnp.exp(-summed))).astype(BF16)


def spread(values, heads, size):
    lane = lax.broadcasted_iota(jnp.int32, (values.shape[0], heads * size), 1)
    wide = jnp.broadcast_to(values[:, heads - 1 : heads], lane.shape)
    for h in range(heads - 2, -1, -1):
        wide = jnp.where(lane < (h + 1) * size, values[:, h : h + 1], wide)
    return wide


def layer_kernel(
    planes, heads, x_ref, bc_ref, dt_ref, xt_ref, bct_ref, taps_x, taps_bc, bias, rate, skip, gain, first, steer, steer_all, out_ref,
    x_pad, bc_pad, x_conv, bc_conv, s_keep, dt_keep, states, logs, y_keep, state_out, total_out, state_in, total_in,
    normed, partial, normed_in, partial_in, send_sem, state_sem, total_sem, normed_sem, partial_sem,
):
    seq, core = lax.axis_index("seq"), lax.axis_index("tp")
    plane, member = lax.div(seq, PLANE), lax.rem(seq, PLANE)
    base = plane * PLANE
    rows, channels = x_ref.shape
    size = channels // heads
    blocks = rows // GROUP
    per_member = blocks // PLANE

    barrier = pltpu.get_barrier_semaphore()
    near = [lax.rem(member + j, PLANE) for j in range(PLANE)]
    far = [lax.rem(plane + j, planes) for j in range(planes)]
    friends = [(base + near[j], core) for j in range(1, PLANE)] + [(base + near[j], 1 - core) for j in range(PLANE)]
    friends = friends + [(far[j] * PLANE + member, core) for j in range(1, planes)]
    for friend in friends:
        pl.semaphore_signal(barrier, inc=1, device_id=friend, device_id_type=MESH)

    x_pad[0:TAIL, :] = xt_ref[...].astype(F32)
    x_pad[TAIL:, :] = x_ref[...].astype(F32)
    for c in range(2):
        bc_pad[0:TAIL, c * N : (c + 1) * N] = bct_ref[c].astype(F32)
        bc_pad[TAIL:, c * N : (c + 1) * N] = bc_ref[c].astype(F32)
    row = lax.broadcasted_iota(jnp.int32, (GROUP, GROUP), 0)
    column = lax.broadcasted_iota(jnp.int32, (GROUP, GROUP), 1)
    causal = row >= column
    lower = causal.astype(BF16)

    def here(at):
        return pl.ds(pl.multiple_of(at * GROUP, GROUP), GROUP)

    def advance(at, carry):
        state, log = carry
        x = smooth(x_pad, at, taps_x[...])
        bc = smooth(bc_pad, at, taps_bc[...])
        x_conv[here(at), :] = x
        bc_conv[here(at), :] = bc
        raw = dt_ref[here(at), :] + bias[...]
        dt = jnp.maximum(raw, 0.0) + jnp.log1p(jnp.exp(-jnp.abs(raw)))
        a = -dt * rate[...]
        one = a.astype(BF16)
        rest = a - one.astype(F32)
        two = rest.astype(BF16)
        three = (rest - two.astype(F32)).astype(BF16)
        s = dot(lower, one) + (dot(lower, two) + dot(lower, three))
        s_keep[here(at), :] = s
        dt_keep[here(at), :] = dt
        states[at] = state
        logs[at] = log
        end = s[GROUP - 1 : GROUP, :]
        weight = spread(jnp.exp(end - s) * dt, heads, size)
        scaled = (x.astype(F32) * weight).astype(BF16)
        b_turned = bc[:, :N].astype(F32).T.astype(BF16)
        ended = spread(jnp.broadcast_to(end, (8, GROUP)), heads, size)
        state = jnp.exp(ended[0:1, :]) * state + dot(b_turned, scaled)
        return state, log + ended

    state, log = lax.fori_loop(0, blocks, advance, (jnp.zeros((N, channels), F32), jnp.zeros((8, channels), F32)))
    state_out[...] = state.astype(BF16)
    total_out[...] = log
    pl.semaphore_wait(barrier, len(friends))

    started = []

    def remote(source, target, sem, device):
        return pltpu.make_async_remote_copy(
            src_ref=source, dst_ref=target, send_sem=send_sem.at[len(started)], recv_sem=sem,
            device_id=device, device_id_type=MESH,
        )

    def send(*what):
        copy = remote(*what)
        copy.start()
        started.append(copy)

    for j in range(1, planes):
        other = (far[j] * PLANE + member, core)
        send(state_out, state_in.at[planes - j], state_sem.at[planes - j], other)
        send(total_out, total_in.at[planes - j], total_sem.at[planes - j], other)

    def inside(at, _):
        x = x_conv[here(at), :]
        bc = bc_conv[here(at), :]
        s = s_keep[here(at), :]
        s_turned = s.T
        dt_turned = dt_keep[here(at), :].T
        scores = lax.dot_general(bc[:, N:], bc[:, :N], (((1,), (1,)), ((), ())), preferred_element_type=F32)
        parts = []
        for h in range(heads):
            differ = s[:, h : h + 1] - s_turned[h : h + 1, :]
            decays = jnp.where(causal, jnp.exp(jnp.where(causal, differ, 0.0)), 0.0)
            mixing = (scores * decays * dt_turned[h : h + 1, :]).astype(BF16)
            parts.append(dot(mixing, x[:, h * size : (h + 1) * size]))
        y_keep[here(at), :] = jnp.concatenate(parts, 1) + skip[...] * x.astype(F32)
        return 0

    lax.fori_loop(0, blocks, inside, 0)

    for j in range(1, planes):
        other = (far[j] * PLANE + member, core)
        remote(state_out, state_in.at[j], state_sem.at[j], other).wait_recv()
        remote(total_out, total_in.at[j], total_sem.at[j], other).wait_recv()
    entering = first[...]
    for j in range(1, planes):
        later = jnp.exp(total_in[j][0:1, :]) * entering + state_in[j].astype(F32)
        entering = jnp.where(far[j] < plane, later, entering)

    same = lax.broadcasted_iota(jnp.int32, (channels, channels), 0) // size == lax.broadcasted_iota(jnp.int32, (channels, channels), 1) // size
    same = same.astype(BF16)

    def finish(at):
        s = s_keep[here(at), :]
        c = bc_conv[here(at), :][:, N:]
        state = states[at] + jnp.exp(logs[at][0:1, :]) * entering
        y = y_keep[here(at), :] + jnp.exp(spread(s, heads, size)) * split_dot(c, state)
        square = y * y
        high = square.astype(BF16)
        low = (square - high.astype(F32)).astype(BF16)
        mean = (dot(high, same) + dot(low, same)) * (1.0 / size)
        scaled = y * lax.rsqrt(mean + EPSILON) * gain[...]
        normed[here(at), :] = scaled.astype(BF16)
        along = jnp.sum(scaled * steer[...], axis=1, keepdims=True)
        partial[at] = jnp.broadcast_to(along, (GROUP, GROUP)).T[0:8, :]

    own_rows = rows // PLANE
    for j in list(range(1, PLANE)) + [0]:
        target = near[j]
        lax.fori_loop(0, per_member, lambda i, _: (finish(target * per_member + i), 0)[1], 0)
        pieces = partial.at[pl.ds(target * per_member, per_member)]
        back = (PLANE - j) % PLANE
        if j:
            chunk = normed.at[pl.ds(pl.multiple_of(target * own_rows, own_rows), own_rows)]
            send(chunk, normed_in.at[member], normed_sem.at[back], (base + target, core))
            send(pieces, partial_in.at[0, back], partial_sem.at[0, back], (base + target, core))
        send(pieces, partial_in.at[1, back], partial_sem.at[1, back], (base + target, 1 - core))
    mine = pl.ds(pl.multiple_of(member * own_rows, own_rows), own_rows)
    normed_in[member] = normed[mine, :]
    penalty = partial[pl.ds(member * per_member, per_member)]
    for j in range(PLANE):
        other = (base + near[j], 1 - core)
        pieces = partial.at[pl.ds(member * per_member, per_member)]
        if j:
            remote(normed.at[mine], normed_in.at[near[j]], normed_sem.at[j], other).wait_recv()
            remote(pieces, partial_in.at[0, j], partial_sem.at[0, j], other).wait_recv()
            penalty = penalty + partial_in[0, j]
        remote(pieces, partial_in.at[1, j], partial_sem.at[1, j], other).wait_recv()
        penalty = penalty + partial_in[1, j]
    penalty = penalty * (1.0 / (channels * PLANE * lax.axis_size("tp")) ** 0.5)
    for i in range(per_member):
        turned = jnp.broadcast_to(penalty[i][0:1, :], (GROUP, GROUP)).T
        turned = jnp.concatenate([turned] * (channels // GROUP), 1)
        span = pl.ds(i * GROUP, GROUP)
        for j in range(PLANE):
            value = normed_in[j, span, :].astype(F32) - turned * steer_all[:, j * channels : (j + 1) * channels]
            out_ref[j, span, :] = value.astype(BF16)
    for copy in started:
        copy.wait_send()


def per_device(tokens, x_weight, bc_weight, dt_weight, conv_x, conv_bc, dt_bias, decay_rate, d_skip, norm_gain, initial_state, steer):
    planes = lax.axis_size("seq") // PLANE
    member = lax.rem(lax.axis_index("seq"), PLANE)
    own_rows, columns = tokens.shape
    depth, all_channels = x_weight.shape
    all_heads = dt_weight.shape[1]
    channels, heads = all_channels // PLANE, all_heads // PLANE
    size = channels // heads
    rows = own_rows * PLANE
    blocks = rows // GROUP

    steps_w = dt_weight.T.reshape(PLANE, heads, depth)
    steps_w = jnp.pad(steps_w, ((0, 0), (0, TAIL - heads), (0, channels + 128 - depth)))
    wide = x_weight.reshape(depth, PLANE, channels).transpose(1, 0, 2)
    wide = jnp.concatenate([wide, jnp.broadcast_to(bc_weight[None], (PLANE,) + bc_weight.shape)], 2)
    pack = jnp.concatenate([wide, steps_w], 1)

    vmem = pl.BlockSpec(memory_space=pltpu.VMEM)
    anywhere = pl.BlockSpec(memory_space=pl.ANY)
    shape = jax.ShapeDtypeStruct
    dma = pltpu.SemaphoreType.DMA
    x_pre, bc_pre, dt_raw, x_tail, bc_tail = pl.pallas_call(
        functools.partial(gather_kernel, planes),
        out_shape=(
            shape((rows, channels), BF16), shape((2, rows, 128), BF16), shape((rows, 128), F32),
            shape((TAIL, channels), BF16), shape((2, TAIL, 128), BF16),
        ),
        in_specs=[anywhere, anywhere],
        out_specs=[vmem] * 5,
        scratch_shapes=[
            pltpu.VMEM((2, rows, columns), BF16),
            pltpu.VMEM((planes, PLANE, depth + TAIL, channels + 128), BF16),
            pltpu.VMEM((rows, channels), BF16),
            pltpu.VMEM((2, rows, 128), BF16),
            pltpu.VMEM((TAIL, channels), BF16),
            pltpu.VMEM((2, TAIL, 128), BF16),
            dma((23 + 8 * planes,)),
            dma((6,)),
            dma((4, 2)),
            dma((4,)),
            dma((2, planes, 4)),
            dma((4,)),
            dma((2,)),
        ],
        compiler_params=pltpu.CompilerParams(collective_id=0, has_side_effects=True, vmem_limit_bytes=48 * 2**20),
    )(tokens, pack)

    def mine(value, axis=0):
        count = value.shape[axis] // PLANE
        return lax.dynamic_slice_in_dim(value, member * count, count, axis)

    def lanes(value):
        return jnp.pad(mine(value), (0, 128 - heads))[None, :]

    first = mine(initial_state).reshape(channels, N).T
    out = pl.pallas_call(
        functools.partial(layer_kernel, planes, heads),
        out_shape=shape((PLANE, own_rows, channels), BF16),
        in_specs=[vmem] * 14,
        out_specs=vmem,
        scratch_shapes=[
            pltpu.VMEM((rows + TAIL, channels), F32),
            pltpu.VMEM((rows + TAIL, 2 * N), F32),
            pltpu.VMEM((rows, channels), BF16),
            pltpu.VMEM((rows, 2 * N), BF16),
            pltpu.VMEM((rows, 128), F32),
            pltpu.VMEM((rows, 128), F32),
            pltpu.VMEM((blocks, N, channels), F32),
            pltpu.VMEM((blocks, 8, channels), F32),
            pltpu.VMEM((rows, channels), F32),
            pltpu.VMEM((N, channels), BF16),
            pltpu.VMEM((8, channels), F32),
            pltpu.VMEM((planes, N, channels), BF16),
            pltpu.VMEM((planes, 8, channels), F32),
            pltpu.VMEM((rows, channels), BF16),
            pltpu.VMEM((blocks, 8, GROUP), F32),
            pltpu.VMEM((PLANE, own_rows, channels), BF16),
            pltpu.VMEM((2, PLANE, blocks // PLANE, 8, GROUP), F32),
            dma((2 * planes + 3 * PLANE,)),
            dma((planes,)),
            dma((planes,)),
            dma((PLANE,)),
            dma((2, PLANE)),
        ],
        compiler_params=pltpu.CompilerParams(collective_id=1, has_side_effects=True, vmem_limit_bytes=48 * 2**20),
    )(
        x_pre, bc_pre, dt_raw, x_tail, bc_tail, mine(conv_x, 1), conv_bc, lanes(dt_bias), lanes(decay_rate),
        jnp.repeat(mine(d_skip), size)[None, :], mine(norm_gain)[None, :], first, mine(steer)[None, :], steer[None, :],
    )
    return out.transpose(1, 0, 2).reshape(own_rows, all_channels)


def solution(mesh):
    placed = (
        P("seq", "tp"),
        P("seq", "tp"),
        P("seq", "tp"),
        P("seq", "tp"),
        P(None, "tp"),
        P(),
        P("tp"),
        P("tp"),
        P("tp"),
        P("tp"),
        P("tp", None, None),
        P("tp"),
    )
    planar = mesh.shape["tp"] == 2 and mesh.shape["seq"] % PLANE == 0
    return jax.shard_map(
        per_device if planar else portable, mesh=mesh, in_specs=placed, out_specs=P("seq", "tp"), check_vma=False
    )
```

```python
import functools

import jax
import jax.numpy as jnp
from jax import lax
from jax.experimental import pallas as pl
from jax.experimental.pallas import tpu as pltpu
from jax.sharding import PartitionSpec as P

MESH = pl.DeviceIdType.MESH
PLANE = 4
TAIL = 16
F32 = jnp.float32
BF16 = jnp.bfloat16

N = 128
GROUP = 128


EPSILON = 1e-05


def passed_along(value, axis, steps):
    count = lax.axis_size(axis)
    first, last = (max(0, -steps), min(count, count - steps))
    return lax.ppermute(value, axis, [(source, source + steps) for source in range(first, last)])


def prefix(x, axis, combine, identity):
    count, mine = (lax.axis_size(axis), lax.axis_index(axis))
    everything = jax.tree.map(
        lambda part, kind: lax.all_gather(part.astype(kind), axis), x, (jnp.bfloat16, jnp.bfloat16)
    )
    start = jax.tree.map(
        lambda part, zero: jnp.broadcast_to(jnp.asarray(zero, part.dtype), part.shape), x, identity
    )

    def turn(k, before):
        reached = k < mine
        new = combine(
            before, jax.tree.map(lambda part, own: part[k].astype(own.dtype), everything, x)
        )
        return jax.tree.map(lambda a, b: jnp.where(reached, a, b), new, before)

    return lax.fori_loop(0, count, turn, start)


def convolve(extended, kernel):
    kernel_rows = kernel.shape[0]
    length = extended.shape[0] - kernel_rows + 1
    summed = kernel[0] * extended[0:length].astype(jnp.float32)
    for offset in range(1, kernel_rows):
        summed = summed + kernel[offset] * extended[offset : offset + length].astype(jnp.float32)
    return jax.nn.silu(summed).astype(jnp.bfloat16)


def block_update(carry_state, inputs):
    x_block, b_block, c_block, a_block, dt_block = inputs
    length = a_block.shape[0]
    cumulative = jnp.cumsum(a_block, axis=0)
    scores = jnp.dot(c_block, b_block.T, preferred_element_type=jnp.float32)
    causal = lax.broadcasted_iota(jnp.int32, (length, length), 0) >= lax.broadcasted_iota(
        jnp.int32, (length, length), 1
    )
    differ = cumulative[:, None, :] - cumulative[None, :, :]
    decays = jnp.where(causal[:, :, None], jnp.exp(jnp.where(causal[:, :, None], differ, 0.0)), 0.0)
    mixing = (scores[:, :, None] * decays * dt_block[None, :, :]).astype(jnp.bfloat16)
    inside = jnp.einsum("tsh,shp->thp", mixing, x_block, preferred_element_type=jnp.float32)
    carried_in = jnp.einsum(
        "tn,hpn->thp", c_block.astype(jnp.float32), carry_state, precision=lax.Precision.HIGHEST
    )
    outputs = inside + jnp.exp(cumulative)[:, :, None] * carried_in
    to_end = jnp.exp(cumulative[-1][None, :] - cumulative) * dt_block
    scaled = (x_block.astype(jnp.float32) * to_end[:, :, None]).astype(jnp.bfloat16)
    added_state = jnp.einsum("shp,sn->hpn", scaled, b_block, preferred_element_type=jnp.float32)
    return (jnp.exp(cumulative[-1])[:, None, None] * carry_state + added_state, outputs)


def combine_carry(earlier, later):
    return (earlier[0] * later[0], later[0][:, None, None] * earlier[1] + later[1])


def portable(
    tokens,
    x_weight,
    bc_weight,
    dt_weight,
    conv_x,
    conv_bc,
    dt_bias,
    decay_rate,
    d_skip,
    norm_gain,
    initial_state,
    steer,
):
    features = lax.all_gather(tokens, "tp", axis=1, tiled=True)
    rim_rows = conv_x.shape[0] - 1
    local_tokens = features.shape[0]
    head_count = dt_weight.shape[1]
    channels = x_weight.shape[1]
    head_size = channels // head_count
    bc_panel = lax.all_gather(bc_weight, "tp", axis=1, tiled=True)
    previous = passed_along(features[local_tokens - rim_rows :], "seq", 1)
    source = jnp.concatenate([previous, features], 0)
    x_sums = jnp.dot(
        source,
        lax.all_gather(x_weight, "seq", axis=0, tiled=True),
        preferred_element_type=jnp.float32,
    )
    bc_sums = jnp.dot(
        source,
        lax.all_gather(bc_panel, "seq", axis=0, tiled=True),
        preferred_element_type=jnp.float32,
    )
    dt_sums = jnp.dot(
        source,
        lax.all_gather(dt_weight, "seq", axis=0, tiled=True),
        preferred_element_type=jnp.float32,
    )
    x_pre = x_sums.astype(jnp.bfloat16)
    bc_pre = bc_sums.astype(jnp.bfloat16)
    dt_raw = dt_sums[rim_rows:]
    x_conv = convolve(x_pre, conv_x)
    bc_conv = convolve(bc_pre, conv_bc)
    b_values = bc_conv[:, :N]
    c_values = bc_conv[:, N:]
    step_size = jax.nn.softplus(dt_raw + dt_bias[None, :])
    log_decay = -step_size * decay_rate[None, :]
    blocks = local_tokens // GROUP
    x_heads = x_conv.reshape(local_tokens, head_count, head_size)
    inputs = (
        x_heads.reshape(blocks, GROUP, head_count, head_size),
        b_values.reshape(blocks, GROUP, N),
        c_values.reshape(blocks, GROUP, N),
        log_decay.reshape(blocks, GROUP, head_count),
        step_size.reshape(blocks, GROUP, head_count),
    )
    zero_state = jnp.zeros((head_count, head_size, N), jnp.float32)
    local_state, local_out = lax.scan(block_update, zero_state, inputs)
    running = jnp.cumsum(log_decay, axis=0)
    local_decay = jnp.exp(running[-1])
    identity = (
        jnp.ones((head_count,), jnp.float32),
        jnp.zeros((head_count, head_size, N), jnp.float32),
    )
    prefix_decay, prefix_state = prefix((local_decay, local_state), "seq", combine_carry, identity)
    entering = prefix_decay[:, None, None] * initial_state + prefix_state
    from_entering = jnp.einsum(
        "tn,hpn->thp", c_values.astype(jnp.float32), entering, precision=lax.Precision.HIGHEST
    )
    outputs = (
        local_out.reshape(local_tokens, head_count, head_size)
        + jnp.exp(running)[:, :, None] * from_entering
        + d_skip[None, :, None] * x_heads.astype(jnp.float32)
    )
    mean_square = jnp.mean(outputs * outputs, axis=-1, keepdims=True)
    normed = (outputs * lax.rsqrt(mean_square + EPSILON)).reshape(
        local_tokens, channels
    ) * norm_gain[None, :]
    partial_dot = jnp.sum(normed * steer[None, :], axis=1)
    total_dot = lax.psum(partial_dot, "tp")
    penalty = total_dot / jnp.sqrt(jnp.float32(channels * lax.axis_size("tp")))
    return (normed - penalty[:, None] * steer[None, :]).astype(jnp.bfloat16)


def dot(a, b):
    return jnp.dot(a, b, preferred_element_type=F32)


def split_dot(a, b):
    high = b.astype(BF16)
    low = (b - high.astype(F32)).astype(BF16)
    return dot(a, high) + dot(a, low)


def smooth(ref, at, taps):
    rows = ref[pl.ds(pl.multiple_of(at * GROUP + TAIL - 8, 8), GROUP + 8), :]
    width = taps.shape[0]
    summed = taps[0:1, :] * rows[9 - width : 9 - width + GROUP]
    for k in range(1, width):
        summed = summed + taps[k : k + 1, :] * rows[9 - width + k : 9 - width + k + GROUP]
    return (summed / (1.0 + jnp.exp(-summed))).astype(BF16)


def spread(values, heads, size):
    lane = lax.broadcasted_iota(jnp.int32, (values.shape[0], heads * size), 1)
    wide = jnp.broadcast_to(values[:, heads - 1 : heads], lane.shape)
    for h in range(heads - 2, -1, -1):
        wide = jnp.where(lane < (h + 1) * size, values[:, h : h + 1], wide)
    return wide


def layer_kernel(
    planes, heads, tok_ref, xw_ref, pack_ref, taps_x, taps_bc, small, gain, first, steer, out_ref,
    toks, weights, wide, narrow, x_tail, x_last, bc_own, bc_all, bc_tail,
    x_pad, bc_pad, x_conv, bc_conv, s_keep, dt_keep, states, logs, y_keep, state_out, total_out, state_in, total_in,
    normed, partial, normed_in, partial_in,
    send_sem, tok_sem, sib_sem, swap_sem, line_sem, own_sem, tail_sem, bct_sem, bc_sem, state_sem, total_sem, normed_sem, partial_sem,
):
    seq, core = lax.axis_index("seq"), lax.axis_index("tp")
    plane, member = lax.div(seq, PLANE), lax.rem(seq, PLANE)
    base = plane * PLANE
    own_rows, columns = tok_ref.shape
    rows = own_rows * PLANE
    half = own_rows // 2
    depth = xw_ref.shape[0]
    channels = weights.shape[3]
    size = channels // heads
    quarter = weights.shape[2] - depth - TAIL
    blocks = rows // GROUP
    per_member = blocks // PLANE
    my_x, my_y = lax.rem(member, 2), lax.div(member, 2)

    def member_at(j):
        return lax.rem(my_y + j // 2, 2) * 2 + lax.rem(my_x + j % 2, 2)

    members = [member_at(j) for j in range(PLANE)]
    far = [lax.rem(plane + j, planes) for j in range(planes)]
    has_below, has_above = plane > 0, plane < planes - 1

    barrier = pltpu.get_barrier_semaphore()

    def greet(s, c):
        pl.semaphore_signal(barrier, inc=1, device_id=(s, c), device_id_type=MESH)

    for j in range(PLANE):
        greet(base + members[j], 1 - core)
        if j:
            greet(base + members[j], core)

    @pl.when(has_below)
    def _():
        for m in range(PLANE):
            for c in range(2):
                greet(base - PLANE + m, c)

    @pl.when(has_above)
    def _():
        for m in range(PLANE):
            for c in range(2):
                greet(base + PLANE + m, c)

    greeted = 2 * PLANE - 1 + jnp.where(has_below, 2 * PLANE, 0) + jnp.where(has_above, 2 * PLANE, 0)
    for j in range(1, planes):
        distant = jnp.abs(far[j] - plane) > 1
        pl.when(distant)(lambda j=j: greet(far[j] * PLANE + member, core))
        greeted = greeted + jnp.where(distant, 1, 0)
    pl.semaphore_wait(barrier, greeted)

    started = []

    def send(source, target, sem, device, when=None):
        copy = pltpu.make_async_remote_copy(
            src_ref=source, dst_ref=target, send_sem=send_sem.at[len(started)], recv_sem=sem,
            device_id=device, device_id_type=MESH,
        )
        started.append((copy, when))
        if when is None:
            copy.start()
        else:
            pl.when(when)(lambda: copy.start())

    def arrived(target, sem, when=None):
        copy = pltpu.make_async_remote_copy(
            src_ref=target, dst_ref=target, send_sem=send_sem.at[0], recv_sem=sem,
            device_id=(seq, 1 - core), device_id_type=MESH,
        )
        if when is None:
            copy.wait_recv()
        else:
            pl.when(when)(lambda: copy.wait_recv())

    def piece(c, j, h):
        return toks.at[c, pl.ds(pl.multiple_of(members[j] * own_rows + h * half, half), half)]

    def own_piece(h):
        return tok_ref.at[pl.ds(h * half, half)]

    def block(p, j):
        return weights.at[p, members[j]]

    across = [(base + members[j], core) for j in range(PLANE)]
    up, down, sibling = (seq + PLANE, core), (seq - PLANE, core), (seq, 1 - core)

    def quarter_of(m):
        return xw_ref.at[:, pl.ds(pl.multiple_of(m * channels, channels), channels)]

    def both(m, slot, sem, device, when=None):
        send(quarter_of(m), weights.at[plane, slot, pl.ds(0, depth)], sem, device, when)
        send(pack_ref.at[m], weights.at[plane, slot, pl.ds(depth, quarter + TAIL)], sem, device, when)

    own_copies = [
        pltpu.make_async_copy(quarter_of(member), weights.at[plane, member, pl.ds(0, depth)], own_sem.at[0]),
        pltpu.make_async_copy(pack_ref.at[member], weights.at[plane, member, pl.ds(depth, quarter + TAIL)], own_sem.at[1]),
        pltpu.make_async_copy(tok_ref, toks.at[core, pl.ds(pl.multiple_of(member * own_rows, own_rows), own_rows)], own_sem.at[2]),
    ]
    for copy in own_copies:
        copy.start()
    for j in (1, 2, 3):
        both(members[j], member, swap_sem.at[j], across[j])
    both(member, member, line_sem.at[0, 1, 0], up, has_above)
    both(member, member, line_sem.at[1, 1, 0], down, has_below)
    send(own_piece(0), piece(core, 0, 0), tok_sem.at[0], across[1])
    send(own_piece(1), piece(core, 0, 1), tok_sem.at[2], across[2])
    send(own_piece(1), piece(core, 0, 1), tok_sem.at[1], across[1])
    send(own_piece(0), piece(core, 0, 0), tok_sem.at[3], across[2])
    send(own_piece(0), piece(core, 0, 0), sib_sem.at[0, 0], sibling)
    send(own_piece(1), piece(core, 0, 1), sib_sem.at[0, 1], sibling)
    for j in (1, 2, 3):
        arrived(block(plane, j), swap_sem.at[j])
        send(block(plane, j), block(plane, j), line_sem.at[0, 1, j], up, has_above)
        send(block(plane, j), block(plane, j), line_sem.at[1, 1, j], down, has_below)

    def relay(step, j):
        lower, upper = plane - step, plane + step
        arrived(block(jnp.maximum(lower, 0), j), line_sem.at[0, step, j], lower >= 0)
        arrived(block(jnp.minimum(upper, planes - 1), j), line_sem.at[1, step, j], upper < planes)
        if step < planes - 1:
            low = block(jnp.maximum(lower, 0), j)
            high = block(jnp.minimum(upper, planes - 1), j)
            send(low, low, line_sem.at[0, step + 1, j], up, jnp.logical_and(lower >= 0, has_above))
            send(high, high, line_sem.at[1, step + 1, j], down, jnp.logical_and(upper < planes, has_below))

    def token(j, h, index, forward=None):
        here = piece(core, j, h)
        arrived(here, tok_sem.at[index])
        if forward is not None:
            send(here, here, tok_sem.at[forward[0]], across[forward[1]])
        send(here, here, sib_sem.at[j, h], sibling)

    def from_sibling(j):
        for h in range(2):
            arrived(piece(1 - core, j, h), sib_sem.at[j, h])

    filler = jnp.zeros((128 - quarter - TAIL, depth), BF16)

    def multiply(j, p):
        where = pl.ds(pl.multiple_of(member_at(j) * own_rows, own_rows), own_rows)
        per_core = columns // (PLANE * depth)
        side = p // per_core
        total_wide, total_narrow = wide[where, :], narrow[where, :]
        for k in range(PLANE):
            span = pl.ds(pl.multiple_of((p % per_core) * (PLANE * depth) + k * depth, depth), depth)
            left = toks[side, where, span]
            total_wide += dot(left, weights[p, k, 0:depth, :])
            turned = jnp.concatenate([weights[p, k, depth:, :], filler], 0)
            total_narrow += lax.dot_general(left, turned, (((1,), (1,)), ((), ())), preferred_element_type=F32)
        wide[where, :] = total_wide
        narrow[where, :] = total_narrow

    def multiply_all(parts, lowest, highest):
        first_part, last_part = parts

        def at(j, _):
            return lax.fori_loop(lowest, highest, lambda p, _: (multiply(j, p), 0)[1], 0)

        lax.fori_loop(first_part, last_part, at, 0)

    wide[...] = jnp.zeros_like(wide)
    narrow[...] = jnp.zeros_like(narrow)
    takes = [
        (1, 0, 0, (4, 2)), (2, 1, 2, (5, 1)), (1, 1, 1, None), (2, 0, 3, None),
    ]
    places = [3, 3, 6, 6]
    near_low, near_high = jnp.maximum(plane - (planes - 2), 0), jnp.minimum(plane + planes - 1, planes)
    steps = [(step, j) for step in range(1, planes) for j in range(PLANE)]
    for at, (step, j) in enumerate(steps):
        for take, place in zip(takes, places):
            if min(place, len(steps) - 1) == at:
                token(*take)
        if at == len(steps) - PLANE + 1:
            for copy in own_copies:
                copy.wait()
            for i in range(3):
                from_sibling(i)
            multiply_all((0, 3), near_low, near_high)
        relay(step, j)
    token(3, 0, 4)
    token(3, 1, 5)
    multiply_all((0, 3), 0, near_low)
    multiply_all((0, 3), near_high, planes)
    from_sibling(3)
    multiply_all((3, 4), 0, planes)

    x_last[...] = wide[rows - TAIL : rows, :].astype(BF16)
    send(x_last, x_tail, tail_sem, up, has_above)
    me = core * PLANE + member
    for i in range(PLANE):
        part = rows // PLANE
        bc_own[:, i * part : (i + 1) * part] = narrow[i * part : (i + 1) * part, :].T[0:quarter, :].astype(BF16)
    for j in range(PLANE):
        for c in (core, 1 - core):
            if j or c is not core:
                send(bc_own, bc_all.at[me], bc_sem.at[me], (base + members[j], c))
    last = bc_own.at[:, pl.ds(rows - GROUP, GROUP)]
    for m in range(PLANE):
        for c in range(2):
            send(last, bc_tail.at[me], bct_sem.at[me], (base + PLANE + m, c), has_above)
    bc_all[me] = bc_own[...]

    mine = pl.ds(pl.multiple_of(member * channels, channels), channels)
    own_small = pltpu.roll(small[...], lax.rem(128 - member * heads, 128), 1)
    bias, rate = own_small[0:1, :], own_small[1:2, :]
    skip = spread(own_small, heads, size)[2:3, :]
    taps = taps_x[:, mine]
    own_gain, own_steer = gain[:, mine], steer[:, mine]
    row = lax.broadcasted_iota(jnp.int32, (GROUP, GROUP), 0)
    column = lax.broadcasted_iota(jnp.int32, (GROUP, GROUP), 1)
    causal = row >= column
    lower = causal.astype(BF16)

    def here(at):
        return pl.ds(pl.multiple_of(at * GROUP, GROUP), GROUP)

    def steps_of(at, _):
        raw = pltpu.roll(narrow[here(at), :], 128 - quarter, 1) + bias
        dt = jnp.maximum(raw, 0.0) + jnp.log1p(jnp.exp(-jnp.abs(raw)))
        a = -dt * rate
        one = a.astype(BF16)
        rest = a - one.astype(F32)
        two = rest.astype(BF16)
        three = (rest - two.astype(F32)).astype(BF16)
        s_keep[here(at), :] = dot(lower, one) + (dot(lower, two) + dot(lower, three))
        dt_keep[here(at), :] = dt
        x_pad[pl.ds(pl.multiple_of(at * GROUP + TAIL, TAIL), GROUP), :] = wide[here(at), :].astype(BF16).astype(F32)
        return 0

    lax.fori_loop(0, blocks, steps_of, 0, unroll=2)

    @pl.when(jnp.logical_not(has_below))
    def _():
        x_tail[...] = jnp.zeros_like(x_tail)
        bc_tail[...] = jnp.zeros_like(bc_tail)

    arrived(x_tail, tail_sem, has_below)
    x_pad[0:TAIL, :] = x_tail[...].astype(F32)

    def convolved(at, _):
        x_conv[here(at), :] = smooth(x_pad, at, taps)
        return 0

    lax.fori_loop(0, blocks, convolved, 0, unroll=2)

    for j in range(PLANE):
        for c in (core, 1 - core):
            if j or c is not core:
                sender = c * PLANE + members[j]
                arrived(bc_all.at[sender], bc_sem.at[sender])
    for sender in range(2 * PLANE):
        arrived(bc_tail.at[sender], bct_sem.at[sender], has_below)
    bc_pad[0:TAIL, :] = bc_tail[...].astype(F32).reshape(2 * N, GROUP).T[GROUP - TAIL :, :]

    def unturned(at, _):
        turned = bc_all[:, :, here(at)].astype(F32).reshape(2 * N, GROUP)
        bc_pad[pl.ds(pl.multiple_of(at * GROUP + TAIL, TAIL), GROUP), :] = turned.T
        return 0

    lax.fori_loop(0, blocks, unturned, 0, unroll=2)

    def advance(at, carry):
        state, log = carry
        bc = smooth(bc_pad, at, taps_bc[...])
        bc_conv[here(at), :] = bc
        s = s_keep[here(at), :]
        states[at] = state
        logs[at] = log
        end = s[GROUP - 1 : GROUP, :]
        weight = spread(jnp.exp(end - s) * dt_keep[here(at), :], heads, size)
        scaled = (x_conv[here(at), :].astype(F32) * weight).astype(BF16)
        b_turned = bc[:, :N].astype(F32).T.astype(BF16)
        ended = spread(jnp.broadcast_to(end, (8, GROUP)), heads, size)
        state = jnp.exp(ended[0:1, :]) * state + dot(b_turned, scaled)
        return state, log + ended

    zeros = (jnp.zeros((N, channels), F32), jnp.zeros((8, channels), F32))
    state, log = lax.fori_loop(0, blocks, advance, zeros, unroll=2)
    state_out[...] = state.astype(BF16)
    total_out[...] = log
    for j in range(1, planes):
        other = (far[j] * PLANE + member, core)
        send(state_out, state_in.at[planes - j], state_sem.at[planes - j], other)
        send(total_out, total_in.at[planes - j], total_sem.at[planes - j], other)

    def inside(at, _):
        x = x_conv[here(at), :]
        bc = bc_conv[here(at), :]
        s = s_keep[here(at), :]
        s_turned = s.T
        dt_turned = dt_keep[here(at), :].T
        scores = lax.dot_general(bc[:, N:], bc[:, :N], (((1,), (1,)), ((), ())), preferred_element_type=F32)
        parts = []
        for h in range(heads):
            differ = s[:, h : h + 1] - s_turned[h : h + 1, :]
            decays = jnp.where(causal, jnp.exp(jnp.where(causal, differ, 0.0)), 0.0)
            mixing = (scores * decays * dt_turned[h : h + 1, :]).astype(BF16)
            parts.append(dot(mixing, x[:, h * size : (h + 1) * size]))
        y_keep[here(at), :] = jnp.concatenate(parts, 1) + skip * x.astype(F32)
        return 0

    lax.fori_loop(0, blocks, inside, 0, unroll=2)

    entering = first[pl.ds(pl.multiple_of(member * channels, channels), channels), :].T
    for j in range(1, planes):
        arrived(state_in.at[j], state_sem.at[j])
        arrived(total_in.at[j], total_sem.at[j])
    for j in range(1, planes):
        later = jnp.exp(total_in[j][0:1, :]) * entering + state_in[j].astype(F32)
        entering = jnp.where(far[j] < plane, later, entering)

    group_of = lax.broadcasted_iota(jnp.int32, (2, channels, channels), 1) // size
    same = (group_of[0] == lax.broadcasted_iota(jnp.int32, (channels, channels), 1) // size).astype(BF16)

    def finish(at):
        s = s_keep[here(at), :]
        c = bc_conv[here(at), :][:, N:]
        state = states[at] + jnp.exp(logs[at][0:1, :]) * entering
        y = y_keep[here(at), :] + jnp.exp(spread(s, heads, size)) * split_dot(c, state)
        square = y * y
        high = square.astype(BF16)
        low = (square - high.astype(F32)).astype(BF16)
        mean = (dot(high, same) + dot(low, same)) * (1.0 / size)
        scaled = y * lax.rsqrt(mean + EPSILON) * own_gain
        normed[here(at), :] = scaled.astype(BF16)
        along = jnp.sum(scaled * own_steer, axis=1, keepdims=True)
        partial[at] = jnp.broadcast_to(along, (GROUP, GROUP)).T[0:8, :]

    for j in (3, 1, 2, 0):
        target = members[j]
        lax.fori_loop(0, per_member, lambda i, _: (finish(target * per_member + i), 0)[1], 0, unroll=2)
        pieces = partial.at[pl.ds(target * per_member, per_member)]
        if j:
            chunk = normed.at[pl.ds(pl.multiple_of(target * own_rows, own_rows), own_rows)]
            send(chunk, normed_in.at[member], normed_sem.at[j], (base + target, core))
            send(pieces, partial_in.at[0, j], partial_sem.at[0, j], (base + target, core))
        send(pieces, partial_in.at[1, j], partial_sem.at[1, j], (base + target, 1 - core))
    normed_in[member] = normed[pl.ds(pl.multiple_of(member * own_rows, own_rows), own_rows), :]
    penalty = partial[pl.ds(member * per_member, per_member)]
    for j in range(PLANE):
        if j:
            arrived(normed_in.at[members[j]], normed_sem.at[j])
            arrived(partial_in.at[0, j], partial_sem.at[0, j])
            penalty = penalty + partial_in[0, j]
        arrived(partial_in.at[1, j], partial_sem.at[1, j])
        penalty = penalty + partial_in[1, j]
    penalty = penalty * (1.0 / (channels * PLANE * lax.axis_size("tp")) ** 0.5)
    for i in range(per_member):
        turned = jnp.broadcast_to(penalty[i][0:1, :], (GROUP, GROUP)).T
        turned = jnp.concatenate([turned] * (channels // GROUP), 1)
        span = pl.ds(i * GROUP, GROUP)
        for j in range(PLANE):
            value = normed_in[j, span, :].astype(F32) - turned * steer[:, j * channels : (j + 1) * channels]
            out_ref[j, span, :] = value.astype(BF16)
    for copy, when in started:
        if when is None:
            copy.wait_send()
        else:
            pl.when(when)(lambda copy=copy: copy.wait_send())


def per_device(tokens, x_weight, bc_weight, dt_weight, conv_x, conv_bc, dt_bias, decay_rate, d_skip, norm_gain, initial_state, steer):
    planes = lax.axis_size("seq") // PLANE
    own_rows, columns = tokens.shape
    depth, all_channels = x_weight.shape
    all_heads = dt_weight.shape[1]
    channels, heads = all_channels // PLANE, all_heads // PLANE
    rows = own_rows * PLANE
    blocks = rows // GROUP
    quarter = bc_weight.shape[1] // PLANE

    steps_w = jnp.pad(dt_weight.T.reshape(PLANE, heads, depth), ((0, 0), (0, TAIL - heads), (0, 0)))
    pack = jnp.concatenate([bc_weight.T.reshape(PLANE, quarter, depth), steps_w], 1)
    small = jnp.pad(jnp.stack([dt_bias, decay_rate, d_skip]), ((0, 5), (0, 128 - all_heads)))

    vmem = pl.BlockSpec(memory_space=pltpu.VMEM)
    anywhere = pl.BlockSpec(memory_space=pl.ANY)
    dma = pltpu.SemaphoreType.DMA
    out = pl.pallas_call(
        functools.partial(layer_kernel, planes, heads),
        out_shape=jax.ShapeDtypeStruct((PLANE, own_rows, channels), BF16),
        in_specs=[anywhere] * 3 + [vmem] * 6,
        out_specs=vmem,
        scratch_shapes=[
            pltpu.VMEM((2, rows, columns), BF16),
            pltpu.VMEM((planes, PLANE, depth + quarter + TAIL, channels), BF16),
            pltpu.VMEM((rows, channels), F32),
            pltpu.VMEM((rows, 128), F32),
            pltpu.VMEM((TAIL, channels), BF16),
            pltpu.VMEM((TAIL, channels), BF16),
            pltpu.VMEM((quarter, rows), BF16),
            pltpu.VMEM((2 * PLANE, quarter, rows), BF16),
            pltpu.VMEM((2 * PLANE, quarter, GROUP), BF16),
            pltpu.VMEM((rows + TAIL, channels), F32),
            pltpu.VMEM((rows + TAIL, 2 * N), F32),
            pltpu.VMEM((rows, channels), BF16),
            pltpu.VMEM((rows, 2 * N), BF16),
            pltpu.VMEM((rows, 128), F32),
            pltpu.VMEM((rows, 128), F32),
            pltpu.VMEM((blocks, N, channels), F32),
            pltpu.VMEM((blocks, 8, channels), F32),
            pltpu.VMEM((rows, channels), F32),
            pltpu.VMEM((N, channels), BF16),
            pltpu.VMEM((8, channels), F32),
            pltpu.VMEM((planes, N, channels), BF16),
            pltpu.VMEM((planes, 8, channels), F32),
            pltpu.VMEM((rows, channels), BF16),
            pltpu.VMEM((blocks, 8, GROUP), F32),
            pltpu.VMEM((PLANE, own_rows, channels), BF16),
            pltpu.VMEM((2, PLANE, blocks // PLANE, 8, GROUP), F32),
            dma((64 + 10 * planes,)),
            dma((6,)),
            dma((PLANE, 2)),
            dma((PLANE,)),
            dma((2, planes, PLANE)),
            dma((3,)),
            dma(()),
            dma((2 * PLANE,)),
            dma((2 * PLANE,)),
            dma((planes,)),
            dma((planes,)),
            dma((PLANE,)),
            dma((2, PLANE)),
        ],
        compiler_params=pltpu.CompilerParams(collective_id=0, has_side_effects=True, vmem_limit_bytes=48 * 2**20),
    )(
        tokens, x_weight, pack, conv_x, conv_bc, small, norm_gain[None, :],
        initial_state.reshape(all_channels, N), steer[None, :],
    )
    return out.transpose(1, 0, 2).reshape(own_rows, all_channels)


def solution(mesh):
    placed = (
        P("seq", "tp"),
        P("seq", "tp"),
        P("seq", "tp"),
        P("seq", "tp"),
        P(None, "tp"),
        P(),
        P("tp"),
        P("tp"),
        P("tp"),
        P("tp"),
        P("tp", None, None),
        P("tp"),
    )
    planar = mesh.shape["tp"] == 2 and mesh.shape["seq"] % PLANE == 0
    return jax.shard_map(
        per_device if planar else portable, mesh=mesh, in_specs=placed, out_specs=P("seq", "tp"), check_vma=False
    )
```

```python
import functools

import jax
import jax.numpy as jnp
from jax import lax
from jax.experimental import pallas as pl
from jax.experimental.pallas import tpu as pltpu
from jax.sharding import PartitionSpec as P

MESH = pl.DeviceIdType.MESH
PLANE = 4
TAIL = 16
F32 = jnp.float32
BF16 = jnp.bfloat16

N = 128
GROUP = 128


EPSILON = 1e-05


def passed_along(value, axis, steps):
    count = lax.axis_size(axis)
    first, last = (max(0, -steps), min(count, count - steps))
    return lax.ppermute(value, axis, [(source, source + steps) for source in range(first, last)])


def prefix(x, axis, combine, identity):
    count, mine = (lax.axis_size(axis), lax.axis_index(axis))
    everything = jax.tree.map(
        lambda part, kind: lax.all_gather(part.astype(kind), axis), x, (jnp.bfloat16, jnp.bfloat16)
    )
    start = jax.tree.map(
        lambda part, zero: jnp.broadcast_to(jnp.asarray(zero, part.dtype), part.shape), x, identity
    )

    def turn(k, before):
        reached = k < mine
        new = combine(
            before, jax.tree.map(lambda part, own: part[k].astype(own.dtype), everything, x)
        )
        return jax.tree.map(lambda a, b: jnp.where(reached, a, b), new, before)

    return lax.fori_loop(0, count, turn, start)


def convolve(extended, kernel):
    kernel_rows = kernel.shape[0]
    length = extended.shape[0] - kernel_rows + 1
    summed = kernel[0] * extended[0:length].astype(jnp.float32)
    for offset in range(1, kernel_rows):
        summed = summed + kernel[offset] * extended[offset : offset + length].astype(jnp.float32)
    return jax.nn.silu(summed).astype(jnp.bfloat16)


def block_update(carry_state, inputs):
    x_block, b_block, c_block, a_block, dt_block = inputs
    length = a_block.shape[0]
    cumulative = jnp.cumsum(a_block, axis=0)
    scores = jnp.dot(c_block, b_block.T, preferred_element_type=jnp.float32)
    causal = lax.broadcasted_iota(jnp.int32, (length, length), 0) >= lax.broadcasted_iota(
        jnp.int32, (length, length), 1
    )
    differ = cumulative[:, None, :] - cumulative[None, :, :]
    decays = jnp.where(causal[:, :, None], jnp.exp(jnp.where(causal[:, :, None], differ, 0.0)), 0.0)
    mixing = (scores[:, :, None] * decays * dt_block[None, :, :]).astype(jnp.bfloat16)
    inside = jnp.einsum("tsh,shp->thp", mixing, x_block, preferred_element_type=jnp.float32)
    carried_in = jnp.einsum(
        "tn,hpn->thp", c_block.astype(jnp.float32), carry_state, precision=lax.Precision.HIGHEST
    )
    outputs = inside + jnp.exp(cumulative)[:, :, None] * carried_in
    to_end = jnp.exp(cumulative[-1][None, :] - cumulative) * dt_block
    scaled = (x_block.astype(jnp.float32) * to_end[:, :, None]).astype(jnp.bfloat16)
    added_state = jnp.einsum("shp,sn->hpn", scaled, b_block, preferred_element_type=jnp.float32)
    return (jnp.exp(cumulative[-1])[:, None, None] * carry_state + added_state, outputs)


def combine_carry(earlier, later):
    return (earlier[0] * later[0], later[0][:, None, None] * earlier[1] + later[1])


def portable(
    tokens,
    x_weight,
    bc_weight,
    dt_weight,
    conv_x,
    conv_bc,
    dt_bias,
    decay_rate,
    d_skip,
    norm_gain,
    initial_state,
    steer,
):
    features = lax.all_gather(tokens, "tp", axis=1, tiled=True)
    rim_rows = conv_x.shape[0] - 1
    local_tokens = features.shape[0]
    head_count = dt_weight.shape[1]
    channels = x_weight.shape[1]
    head_size = channels // head_count
    bc_panel = lax.all_gather(bc_weight, "tp", axis=1, tiled=True)
    previous = passed_along(features[local_tokens - rim_rows :], "seq", 1)
    source = jnp.concatenate([previous, features], 0)
    x_sums = jnp.dot(
        source,
        lax.all_gather(x_weight, "seq", axis=0, tiled=True),
        preferred_element_type=jnp.float32,
    )
    bc_sums = jnp.dot(
        source,
        lax.all_gather(bc_panel, "seq", axis=0, tiled=True),
        preferred_element_type=jnp.float32,
    )
    dt_sums = jnp.dot(
        source,
        lax.all_gather(dt_weight, "seq", axis=0, tiled=True),
        preferred_element_type=jnp.float32,
    )
    x_pre = x_sums.astype(jnp.bfloat16)
    bc_pre = bc_sums.astype(jnp.bfloat16)
    dt_raw = dt_sums[rim_rows:]
    x_conv = convolve(x_pre, conv_x)
    bc_conv = convolve(bc_pre, conv_bc)
    b_values = bc_conv[:, :N]
    c_values = bc_conv[:, N:]
    step_size = jax.nn.softplus(dt_raw + dt_bias[None, :])
    log_decay = -step_size * decay_rate[None, :]
    blocks = local_tokens // GROUP
    x_heads = x_conv.reshape(local_tokens, head_count, head_size)
    inputs = (
        x_heads.reshape(blocks, GROUP, head_count, head_size),
        b_values.reshape(blocks, GROUP, N),
        c_values.reshape(blocks, GROUP, N),
        log_decay.reshape(blocks, GROUP, head_count),
        step_size.reshape(blocks, GROUP, head_count),
    )
    zero_state = jnp.zeros((head_count, head_size, N), jnp.float32)
    local_state, local_out = lax.scan(block_update, zero_state, inputs)
    running = jnp.cumsum(log_decay, axis=0)
    local_decay = jnp.exp(running[-1])
    identity = (
        jnp.ones((head_count,), jnp.float32),
        jnp.zeros((head_count, head_size, N), jnp.float32),
    )
    prefix_decay, prefix_state = prefix((local_decay, local_state), "seq", combine_carry, identity)
    entering = prefix_decay[:, None, None] * initial_state + prefix_state
    from_entering = jnp.einsum(
        "tn,hpn->thp", c_values.astype(jnp.float32), entering, precision=lax.Precision.HIGHEST
    )
    outputs = (
        local_out.reshape(local_tokens, head_count, head_size)
        + jnp.exp(running)[:, :, None] * from_entering
        + d_skip[None, :, None] * x_heads.astype(jnp.float32)
    )
    mean_square = jnp.mean(outputs * outputs, axis=-1, keepdims=True)
    normed = (outputs * lax.rsqrt(mean_square + EPSILON)).reshape(
        local_tokens, channels
    ) * norm_gain[None, :]
    partial_dot = jnp.sum(normed * steer[None, :], axis=1)
    total_dot = lax.psum(partial_dot, "tp")
    penalty = total_dot / jnp.sqrt(jnp.float32(channels * lax.axis_size("tp")))
    return (normed - penalty[:, None] * steer[None, :]).astype(jnp.bfloat16)


def dot(a, b):
    return jnp.dot(a, b, preferred_element_type=F32)


def split_dot(a, b):
    high = b.astype(BF16)
    low = (b - high.astype(F32)).astype(BF16)
    return dot(a, high) + dot(a, low)


def smooth(ref, at, taps):
    rows = ref[pl.ds(pl.multiple_of(at * GROUP + TAIL - 8, 8), GROUP + 8), :]
    width = taps.shape[0]
    summed = taps[0:1, :] * rows[9 - width : 9 - width + GROUP]
    for k in range(1, width):
        summed = summed + taps[k : k + 1, :] * rows[9 - width + k : 9 - width + k + GROUP]
    return (summed / (1.0 + jnp.exp(-summed))).astype(BF16)


def spread(values, heads, size):
    lane = lax.broadcasted_iota(jnp.int32, (values.shape[0], heads * size), 1)
    wide = jnp.broadcast_to(values[:, heads - 1 : heads], lane.shape)
    for h in range(heads - 2, -1, -1):
        wide = jnp.where(lane < (h + 1) * size, values[:, h : h + 1], wide)
    return wide


def layer_kernel(
    planes, heads, tok_ref, xw_ref, bcw_hbm, dtw_hbm, taps_x_hbm, taps_bc_hbm, bias_hbm, rate_hbm, skip_hbm, gain_hbm, first_hbm, steer_hbm, out_ref,
    bcw, dtw, pack_ref, taps_x, taps_bc, small_in, small, gain, first, steer, load_sem,
    toks, weights, wide, narrow, x_tail, x_last, bc_own, bc_all, bc_tail,
    x_pad, bc_pad, x_conv, bc_conv, s_keep, dt_keep, states, logs, y_keep, state_out, total_out, state_in, total_in,
    normed, partial, normed_in, partial_in,
    send_sem, tok_sem, sib_sem, swap_sem, line_sem, own_sem, tail_sem, bct_sem, bc_sem, state_sem, total_sem, normed_sem, partial_sem,
):
    seq, core = lax.axis_index("seq"), lax.axis_index("tp")
    plane, member = lax.div(seq, PLANE), lax.rem(seq, PLANE)
    base = plane * PLANE
    own_rows, columns = tok_ref.shape
    rows = own_rows * PLANE
    half = own_rows // 2
    depth = xw_ref.shape[0]
    channels = weights.shape[3]
    size = channels // heads
    quarter = weights.shape[2] - depth - TAIL
    blocks = rows // GROUP
    per_member = blocks // PLANE
    my_x, my_y = lax.rem(member, 2), lax.div(member, 2)

    def member_at(j):
        return lax.rem(my_y + j // 2, 2) * 2 + lax.rem(my_x + j % 2, 2)

    members = [member_at(j) for j in range(PLANE)]
    far = [lax.rem(plane + j, planes) for j in range(planes)]
    has_below, has_above = plane > 0, plane < planes - 1

    loads = [
        (bcw_hbm, bcw), (dtw_hbm, dtw), (taps_x_hbm, taps_x), (taps_bc_hbm, taps_bc), (bias_hbm, small_in.at[0]),
        (rate_hbm, small_in.at[1]), (skip_hbm, small_in.at[2]), (gain_hbm, gain), (steer_hbm, steer),
        (first_hbm.at[pl.ds(pl.multiple_of(member * channels, channels), channels)], first),
    ]
    loads = [pltpu.make_async_copy(source, target, load_sem.at[i]) for i, (source, target) in enumerate(loads)]
    for copy in loads:
        copy.start()
    barrier = pltpu.get_barrier_semaphore()

    def greet(s, c):
        pl.semaphore_signal(barrier, inc=1, device_id=(s, c), device_id_type=MESH)

    for j in range(PLANE):
        greet(base + members[j], 1 - core)
        if j:
            greet(base + members[j], core)

    @pl.when(has_below)
    def _():
        for m in range(PLANE):
            for c in range(2):
                greet(base - PLANE + m, c)

    @pl.when(has_above)
    def _():
        for m in range(PLANE):
            for c in range(2):
                greet(base + PLANE + m, c)

    greeted = 2 * PLANE - 1 + jnp.where(has_below, 2 * PLANE, 0) + jnp.where(has_above, 2 * PLANE, 0)
    for j in range(1, planes):
        distant = jnp.abs(far[j] - plane) > 1
        pl.when(distant)(lambda j=j: greet(far[j] * PLANE + member, core))
        greeted = greeted + jnp.where(distant, 1, 0)
    pl.semaphore_wait(barrier, greeted)

    started = []

    def send(source, target, sem, device, when=None):
        copy = pltpu.make_async_remote_copy(
            src_ref=source, dst_ref=target, send_sem=send_sem.at[len(started)], recv_sem=sem,
            device_id=device, device_id_type=MESH,
        )
        started.append((copy, when))
        if when is None:
            copy.start()
        else:
            pl.when(when)(lambda: copy.start())

    def arrived(target, sem, when=None):
        copy = pltpu.make_async_remote_copy(
            src_ref=target, dst_ref=target, send_sem=send_sem.at[0], recv_sem=sem,
            device_id=(seq, 1 - core), device_id_type=MESH,
        )
        if when is None:
            copy.wait_recv()
        else:
            pl.when(when)(lambda: copy.wait_recv())

    def piece(c, j, h):
        return toks.at[c, pl.ds(pl.multiple_of(members[j] * own_rows + h * half, half), half)]

    def own_piece(h):
        return tok_ref.at[pl.ds(h * half, half)]

    def block(p, j):
        return weights.at[p, members[j]]

    across = [(base + members[j], core) for j in range(PLANE)]
    up, down, sibling = (seq + PLANE, core), (seq - PLANE, core), (seq, 1 - core)

    def quarter_of(m):
        return xw_ref.at[:, pl.ds(pl.multiple_of(m * channels, channels), channels)]

    def wide_part(m, *where):
        send(quarter_of(m), weights.at[plane, member, pl.ds(0, depth)], *where)

    def thin_part(m, *where):
        send(pack_ref.at[m], weights.at[plane, member, pl.ds(depth, quarter + TAIL)], *where)

    own_copies = [
        pltpu.make_async_copy(quarter_of(member), weights.at[plane, member, pl.ds(0, depth)], own_sem.at[0]),
        pltpu.make_async_copy(pack_ref.at[member], weights.at[plane, member, pl.ds(depth, quarter + TAIL)], own_sem.at[1]),
        pltpu.make_async_copy(tok_ref, toks.at[core, pl.ds(pl.multiple_of(member * own_rows, own_rows), own_rows)], own_sem.at[2]),
    ]
    own_copies[0].start()
    own_copies[2].start()

    def first_parts(part):
        for j in (1, 2, 3):
            part(members[j], swap_sem.at[j], across[j])
        part(member, line_sem.at[0, 1, 0], up, has_above)
        part(member, line_sem.at[1, 1, 0], down, has_below)

    first_parts(wide_part)
    loads[0].wait()
    loads[1].wait()
    turned = bcw[...].astype(F32).T.astype(BF16)
    for m in range(PLANE):
        pack_ref[m, 0:quarter, :] = turned[m * quarter : (m + 1) * quarter]
        pack_ref[m, quarter:, :] = dtw[...]
    own_copies[1].start()
    first_parts(thin_part)
    send(own_piece(0), piece(core, 0, 0), tok_sem.at[0], across[1])
    send(own_piece(1), piece(core, 0, 1), tok_sem.at[2], across[2])
    send(own_piece(1), piece(core, 0, 1), tok_sem.at[1], across[1])
    send(own_piece(0), piece(core, 0, 0), tok_sem.at[3], across[2])
    send(own_piece(0), piece(core, 0, 0), sib_sem.at[0, 0], sibling)
    send(own_piece(1), piece(core, 0, 1), sib_sem.at[0, 1], sibling)
    for j in (1, 2, 3):
        arrived(block(plane, j), swap_sem.at[j])
        send(block(plane, j), block(plane, j), line_sem.at[0, 1, j], up, has_above)
        send(block(plane, j), block(plane, j), line_sem.at[1, 1, j], down, has_below)

    def relay(step, j):
        lower, upper = plane - step, plane + step
        arrived(block(jnp.maximum(lower, 0), j), line_sem.at[0, step, j], lower >= 0)
        arrived(block(jnp.minimum(upper, planes - 1), j), line_sem.at[1, step, j], upper < planes)
        if step < planes - 1:
            low = block(jnp.maximum(lower, 0), j)
            high = block(jnp.minimum(upper, planes - 1), j)
            send(low, low, line_sem.at[0, step + 1, j], up, jnp.logical_and(lower >= 0, has_above))
            send(high, high, line_sem.at[1, step + 1, j], down, jnp.logical_and(upper < planes, has_below))

    def token(j, h, index, forward=None):
        here = piece(core, j, h)
        arrived(here, tok_sem.at[index])
        if forward is not None:
            send(here, here, tok_sem.at[forward[0]], across[forward[1]])
        send(here, here, sib_sem.at[j, h], sibling)

    def from_sibling(j):
        for h in range(2):
            arrived(piece(1 - core, j, h), sib_sem.at[j, h])

    filler = jnp.zeros((128 - quarter - TAIL, depth), BF16)

    def multiply(j, p):
        where = pl.ds(pl.multiple_of(member_at(j) * own_rows, own_rows), own_rows)
        per_core = columns // (PLANE * depth)
        side = p // per_core
        total_wide, total_narrow = wide[where, :], narrow[where, :]
        for k in range(PLANE):
            span = pl.ds(pl.multiple_of((p % per_core) * (PLANE * depth) + k * depth, depth), depth)
            left = toks[side, where, span]
            total_wide += dot(left, weights[p, k, 0:depth, :])
            turned = jnp.concatenate([weights[p, k, depth:, :], filler], 0)
            total_narrow += lax.dot_general(left, turned, (((1,), (1,)), ((), ())), preferred_element_type=F32)
        wide[where, :] = total_wide
        narrow[where, :] = total_narrow

    def multiply_all(parts, lowest, highest):
        first_part, last_part = parts

        def at(j, _):
            return lax.fori_loop(lowest, highest, lambda p, _: (multiply(j, p), 0)[1], 0)

        lax.fori_loop(first_part, last_part, at, 0)

    wide[...] = jnp.zeros_like(wide)
    narrow[...] = jnp.zeros_like(narrow)
    takes = [
        (1, 0, 0, (4, 2)), (2, 1, 2, (5, 1)), (1, 1, 1, None), (2, 0, 3, None),
    ]
    places = [3, 3, 6, 6]
    near_low, near_high = jnp.maximum(plane - (planes - 2), 0), jnp.minimum(plane + planes - 1, planes)
    steps = [(step, j) for step in range(1, planes) for j in range(PLANE)]
    for at, (step, j) in enumerate(steps):
        for take, place in zip(takes, places):
            if min(place, len(steps) - 1) == at:
                token(*take)
        if at == len(steps) - PLANE + 1:
            for copy in own_copies:
                copy.wait()
            for i in range(3):
                from_sibling(i)
            multiply_all((0, 3), near_low, near_high)
        relay(step, j)
    token(3, 0, 4)
    token(3, 1, 5)
    multiply_all((0, 3), 0, near_low)
    multiply_all((0, 3), near_high, planes)
    from_sibling(3)
    multiply_all((3, 4), 0, planes)

    x_last[...] = wide[rows - TAIL : rows, :].astype(BF16)
    send(x_last, x_tail, tail_sem, up, has_above)
    me = core * PLANE + member
    for i in range(PLANE):
        part = rows // PLANE
        bc_own[:, i * part : (i + 1) * part] = narrow[i * part : (i + 1) * part, :].T[0:quarter, :].astype(BF16)
    for j in (3, 1, 2):
        send(bc_own, bc_all.at[me], bc_sem.at[me], across[j])
    send(bc_own, bc_all.at[me], bc_sem.at[me], sibling)
    last = bc_own.at[:, pl.ds(rows - GROUP, GROUP)]
    for m in range(PLANE):
        for c in range(2):
            send(last, bc_tail.at[me], bct_sem.at[me], (base + PLANE + m, c), has_above)
    bc_all[me] = bc_own[...]

    mine = pl.ds(pl.multiple_of(member * channels, channels), channels)
    for copy in loads[2:]:
        copy.wait()
    small[...] = jnp.zeros_like(small)
    for i in range(3):
        small[i : i + 1, 0 : PLANE * heads] = small_in[i]
    own_small = pltpu.roll(small[...], lax.rem(128 - member * heads, 128), 1)
    bias, rate = own_small[0:1, :], own_small[1:2, :]
    skip = spread(own_small, heads, size)[2:3, :]
    taps = taps_x[:, mine]
    own_gain, own_steer = gain[:, mine], steer[:, mine]
    row = lax.broadcasted_iota(jnp.int32, (GROUP, GROUP), 0)
    column = lax.broadcasted_iota(jnp.int32, (GROUP, GROUP), 1)
    causal = row >= column
    lower = causal.astype(BF16)

    def here(at):
        return pl.ds(pl.multiple_of(at * GROUP, GROUP), GROUP)

    def steps_of(at, _):
        raw = pltpu.roll(narrow[here(at), :], 128 - quarter - member * heads, 1) + bias
        dt = jnp.maximum(raw, 0.0) + jnp.log1p(jnp.exp(-jnp.abs(raw)))
        a = -dt * rate
        one = a.astype(BF16)
        rest = a - one.astype(F32)
        two = rest.astype(BF16)
        three = (rest - two.astype(F32)).astype(BF16)
        s_keep[here(at), :] = dot(lower, one) + (dot(lower, two) + dot(lower, three))
        dt_keep[here(at), :] = dt
        x_pad[pl.ds(pl.multiple_of(at * GROUP + TAIL, TAIL), GROUP), :] = wide[here(at), :].astype(BF16).astype(F32)
        return 0

    lax.fori_loop(0, blocks, steps_of, 0, unroll=2)
    for j in (1, 2, 3):
        slot = core * PLANE + members[j]
        arrived(bc_all.at[slot], bc_sem.at[slot])
        send(bc_all.at[slot], bc_all.at[slot], bc_sem.at[slot], sibling)

    @pl.when(jnp.logical_not(has_below))
    def _():
        x_tail[...] = jnp.zeros_like(x_tail)
        bc_tail[...] = jnp.zeros_like(bc_tail)

    arrived(x_tail, tail_sem, has_below)
    x_pad[0:TAIL, :] = x_tail[...].astype(F32)

    def convolved(at, _):
        x_conv[here(at), :] = smooth(x_pad, at, taps)
        return 0

    lax.fori_loop(0, blocks, convolved, 0, unroll=2)

    for j in range(PLANE):
        slot = (1 - core) * PLANE + members[j]
        arrived(bc_all.at[slot], bc_sem.at[slot])
    for sender in range(2 * PLANE):
        arrived(bc_tail.at[sender], bct_sem.at[sender], has_below)
    bc_pad[0:TAIL, :] = bc_tail[...].astype(F32).reshape(2 * N, GROUP).T[GROUP - TAIL :, :]

    def unturned(at, _):
        turned = bc_all[:, :, here(at)].astype(F32).reshape(2 * N, GROUP)
        bc_pad[pl.ds(pl.multiple_of(at * GROUP + TAIL, TAIL), GROUP), :] = turned.T
        return 0

    lax.fori_loop(0, blocks, unturned, 0, unroll=2)

    def advance(at, carry):
        state, log = carry
        bc = smooth(bc_pad, at, taps_bc[...])
        bc_conv[here(at), :] = bc
        s = s_keep[here(at), :]
        states[at] = state
        logs[at] = log
        end = s[GROUP - 1 : GROUP, :]
        weight = spread(jnp.exp(end - s) * dt_keep[here(at), :], heads, size)
        scaled = (x_conv[here(at), :].astype(F32) * weight).astype(BF16)
        b_turned = bc[:, :N].astype(F32).T.astype(BF16)
        ended = spread(jnp.broadcast_to(end, (8, GROUP)), heads, size)
        state = jnp.exp(ended[0:1, :]) * state + dot(b_turned, scaled)
        return state, log + ended

    zeros = (jnp.zeros((N, channels), F32), jnp.zeros((8, channels), F32))
    state, log = lax.fori_loop(0, blocks, advance, zeros, unroll=2)
    state_out[...] = state.astype(BF16)
    total_out[...] = log
    for j in range(1, planes):
        other = (far[j] * PLANE + member, core)
        send(state_out, state_in.at[planes - j], state_sem.at[planes - j], other)
        send(total_out, total_in.at[planes - j], total_sem.at[planes - j], other)

    def inside(at, _):
        x = x_conv[here(at), :]
        bc = bc_conv[here(at), :]
        s = s_keep[here(at), :]
        s_turned = s.T
        dt_turned = dt_keep[here(at), :].T
        scores = lax.dot_general(bc[:, N:], bc[:, :N], (((1,), (1,)), ((), ())), preferred_element_type=F32)
        parts = []
        for h in range(heads):
            differ = s[:, h : h + 1] - s_turned[h : h + 1, :]
            decays = jnp.where(causal, jnp.exp(jnp.where(causal, differ, 0.0)), 0.0)
            mixing = (scores * decays * dt_turned[h : h + 1, :]).astype(BF16)
            parts.append(dot(mixing, x[:, h * size : (h + 1) * size]))
        y_keep[here(at), :] = jnp.concatenate(parts, 1) + skip * x.astype(F32)
        return 0

    lax.fori_loop(0, blocks, inside, 0, unroll=2)

    entering = first[...].T
    for j in range(1, planes):
        arrived(state_in.at[j], state_sem.at[j])
        arrived(total_in.at[j], total_sem.at[j])
    for j in range(1, planes):
        later = jnp.exp(total_in[j][0:1, :]) * entering + state_in[j].astype(F32)
        entering = jnp.where(far[j] < plane, later, entering)

    group_of = lax.broadcasted_iota(jnp.int32, (2, channels, channels), 1) // size
    same = (group_of[0] == lax.broadcasted_iota(jnp.int32, (channels, channels), 1) // size).astype(BF16)

    def finish(at):
        s = s_keep[here(at), :]
        c = bc_conv[here(at), :][:, N:]
        state = states[at] + jnp.exp(logs[at][0:1, :]) * entering
        y = y_keep[here(at), :] + jnp.exp(spread(s, heads, size)) * split_dot(c, state)
        square = y * y
        high = square.astype(BF16)
        low = (square - high.astype(F32)).astype(BF16)
        mean = (dot(high, same) + dot(low, same)) * (1.0 / size)
        scaled = y * lax.rsqrt(mean + EPSILON) * own_gain
        normed[here(at), :] = scaled.astype(BF16)
        along = jnp.sum(scaled * own_steer, axis=1, keepdims=True)
        partial[at] = jnp.broadcast_to(along, (GROUP, GROUP)).T[0:8, :]

    for j in (3, 1, 2, 0):
        target = members[j]
        lax.fori_loop(0, per_member, lambda i, _: (finish(target * per_member + i), 0)[1], 0, unroll=2)
        pieces = partial.at[pl.ds(target * per_member, per_member)]
        if j:
            chunk = normed.at[pl.ds(pl.multiple_of(target * own_rows, own_rows), own_rows)]
            send(chunk, normed_in.at[member], normed_sem.at[j], (base + target, core))
            send(pieces, partial_in.at[0, j], partial_sem.at[0, j], (base + target, core))
        send(pieces, partial_in.at[1, j], partial_sem.at[1, j], (base + target, 1 - core))
    normed_in[member] = normed[pl.ds(pl.multiple_of(member * own_rows, own_rows), own_rows), :]
    penalty = partial[pl.ds(member * per_member, per_member)]
    for j in range(PLANE):
        if j:
            arrived(normed_in.at[members[j]], normed_sem.at[j])
            arrived(partial_in.at[0, j], partial_sem.at[0, j])
            penalty = penalty + partial_in[0, j]
        arrived(partial_in.at[1, j], partial_sem.at[1, j])
        penalty = penalty + partial_in[1, j]
    penalty = penalty * (1.0 / (channels * PLANE * lax.axis_size("tp")) ** 0.5)
    for i in range(per_member):
        turned = jnp.broadcast_to(penalty[i][0:1, :], (GROUP, GROUP)).T
        turned = jnp.concatenate([turned] * (channels // GROUP), 1)
        span = pl.ds(i * GROUP, GROUP)
        for j in range(PLANE):
            value = normed_in[j, span, :].astype(F32) - turned * steer[:, j * channels : (j + 1) * channels]
            out_ref[span, j * channels : (j + 1) * channels] = value.astype(BF16)
    for copy, when in started:
        if when is None:
            copy.wait_send()
        else:
            pl.when(when)(lambda copy=copy: copy.wait_send())


def per_device(tokens, x_weight, bc_weight, dt_weight, conv_x, conv_bc, dt_bias, decay_rate, d_skip, norm_gain, initial_state, steer):
    planes = lax.axis_size("seq") // PLANE
    own_rows, columns = tokens.shape
    depth, all_channels = x_weight.shape
    all_heads = dt_weight.shape[1]
    channels, heads = all_channels // PLANE, all_heads // PLANE
    rows = own_rows * PLANE
    blocks = rows // GROUP
    quarter = bc_weight.shape[1] // PLANE

    vmem = pl.BlockSpec(memory_space=pltpu.VMEM)
    far = pl.BlockSpec(memory_space=pltpu.HBM)
    dma = pltpu.SemaphoreType.DMA
    out = pl.pallas_call(
        functools.partial(layer_kernel, planes, heads),
        out_shape=jax.ShapeDtypeStruct((own_rows, all_channels), BF16),
        in_specs=[far] * 12,
        out_specs=vmem,
        scratch_shapes=[
            pltpu.VMEM(bc_weight.shape, BF16),
            pltpu.VMEM((all_heads, depth), BF16),
            pltpu.VMEM((PLANE, quarter + TAIL, depth), BF16),
            pltpu.VMEM(conv_x.shape, F32),
            pltpu.VMEM(conv_bc.shape, F32),
            pltpu.VMEM((3, 1, all_heads), F32),
            pltpu.VMEM((8, 128), F32),
            pltpu.VMEM((1, all_channels), F32),
            pltpu.VMEM((channels, N), F32),
            pltpu.VMEM((1, all_channels), F32),
            dma((10,)),
            pltpu.VMEM((2, rows, columns), BF16),
            pltpu.VMEM((planes, PLANE, depth + quarter + TAIL, channels), BF16),
            pltpu.VMEM((rows, channels), F32),
            pltpu.VMEM((rows, 128), F32),
            pltpu.VMEM((TAIL, channels), BF16),
            pltpu.VMEM((TAIL, channels), BF16),
            pltpu.VMEM((quarter, rows), BF16),
            pltpu.VMEM((2 * PLANE, quarter, rows), BF16),
            pltpu.VMEM((2 * PLANE, quarter, GROUP), BF16),
            pltpu.VMEM((rows + TAIL, channels), F32),
            pltpu.VMEM((rows + TAIL, 2 * N), F32),
            pltpu.VMEM((rows, channels), BF16),
            pltpu.VMEM((rows, 2 * N), BF16),
            pltpu.VMEM((rows, 128), F32),
            pltpu.VMEM((rows, 128), F32),
            pltpu.VMEM((blocks, N, channels), F32),
            pltpu.VMEM((blocks, 8, channels), F32),
            pltpu.VMEM((rows, channels), F32),
            pltpu.VMEM((N, channels), BF16),
            pltpu.VMEM((8, channels), F32),
            pltpu.VMEM((planes, N, channels), BF16),
            pltpu.VMEM((planes, 8, channels), F32),
            pltpu.VMEM((rows, channels), BF16),
            pltpu.VMEM((blocks, 8, GROUP), F32),
            pltpu.VMEM((PLANE, own_rows, channels), BF16),
            pltpu.VMEM((2, PLANE, blocks // PLANE, 8, GROUP), F32),
            dma((64 + 10 * planes,)),
            dma((6,)),
            dma((PLANE, 2)),
            dma((PLANE,)),
            dma((2, planes, PLANE)),
            dma((3,)),
            dma(()),
            dma((2 * PLANE,)),
            dma((2 * PLANE,)),
            dma((planes,)),
            dma((planes,)),
            dma((PLANE,)),
            dma((2, PLANE)),
        ],
        compiler_params=pltpu.CompilerParams(collective_id=0, has_side_effects=True, vmem_limit_bytes=60 * 2**20),
    )(
        tokens, x_weight, bc_weight, dt_weight.T, conv_x, conv_bc, dt_bias[None, :], decay_rate[None, :], d_skip[None, :],
        norm_gain[None, :], initial_state.reshape(all_channels, N), steer[None, :],
    )
    return out


def solution(mesh):
    placed = (
        P("seq", "tp"),
        P("seq", "tp"),
        P("seq", "tp"),
        P("seq", "tp"),
        P(None, "tp"),
        P(),
        P("tp"),
        P("tp"),
        P("tp"),
        P("tp"),
        P("tp", None, None),
        P("tp"),
    )
    planar = mesh.shape["tp"] == 2 and mesh.shape["seq"] % PLANE == 0
    return jax.shard_map(
        per_device if planar else portable, mesh=mesh, in_specs=placed, out_specs=P("seq", "tp"), check_vma=False
    )
```

```python
import functools

import jax
import jax.numpy as jnp
from jax import lax
from jax.experimental import pallas as pl
from jax.experimental.pallas import tpu as pltpu
from jax.sharding import PartitionSpec as P

MESH = pl.DeviceIdType.MESH
PLANE = 4
TAIL = 16
F32 = jnp.float32
BF16 = jnp.bfloat16

N = 128
GROUP = 128


EPSILON = 1e-05


def passed_along(value, axis, steps):
    count = lax.axis_size(axis)
    first, last = (max(0, -steps), min(count, count - steps))
    return lax.ppermute(value, axis, [(source, source + steps) for source in range(first, last)])


def prefix(x, axis, combine, identity):
    count, mine = (lax.axis_size(axis), lax.axis_index(axis))
    everything = jax.tree.map(
        lambda part, kind: lax.all_gather(part.astype(kind), axis), x, (jnp.bfloat16, jnp.bfloat16)
    )
    start = jax.tree.map(
        lambda part, zero: jnp.broadcast_to(jnp.asarray(zero, part.dtype), part.shape), x, identity
    )

    def turn(k, before):
        reached = k < mine
        new = combine(
            before, jax.tree.map(lambda part, own: part[k].astype(own.dtype), everything, x)
        )
        return jax.tree.map(lambda a, b: jnp.where(reached, a, b), new, before)

    return lax.fori_loop(0, count, turn, start)


def convolve(extended, kernel):
    kernel_rows = kernel.shape[0]
    length = extended.shape[0] - kernel_rows + 1
    summed = kernel[0] * extended[0:length].astype(jnp.float32)
    for offset in range(1, kernel_rows):
        summed = summed + kernel[offset] * extended[offset : offset + length].astype(jnp.float32)
    return jax.nn.silu(summed).astype(jnp.bfloat16)


def block_update(carry_state, inputs):
    x_block, b_block, c_block, a_block, dt_block = inputs
    length = a_block.shape[0]
    cumulative = jnp.cumsum(a_block, axis=0)
    scores = jnp.dot(c_block, b_block.T, preferred_element_type=jnp.float32)
    causal = lax.broadcasted_iota(jnp.int32, (length, length), 0) >= lax.broadcasted_iota(
        jnp.int32, (length, length), 1
    )
    differ = cumulative[:, None, :] - cumulative[None, :, :]
    decays = jnp.where(causal[:, :, None], jnp.exp(jnp.where(causal[:, :, None], differ, 0.0)), 0.0)
    mixing = (scores[:, :, None] * decays * dt_block[None, :, :]).astype(jnp.bfloat16)
    inside = jnp.einsum("tsh,shp->thp", mixing, x_block, preferred_element_type=jnp.float32)
    carried_in = jnp.einsum(
        "tn,hpn->thp", c_block.astype(jnp.float32), carry_state, precision=lax.Precision.HIGHEST
    )
    outputs = inside + jnp.exp(cumulative)[:, :, None] * carried_in
    to_end = jnp.exp(cumulative[-1][None, :] - cumulative) * dt_block
    scaled = (x_block.astype(jnp.float32) * to_end[:, :, None]).astype(jnp.bfloat16)
    added_state = jnp.einsum("shp,sn->hpn", scaled, b_block, preferred_element_type=jnp.float32)
    return (jnp.exp(cumulative[-1])[:, None, None] * carry_state + added_state, outputs)


def combine_carry(earlier, later):
    return (earlier[0] * later[0], later[0][:, None, None] * earlier[1] + later[1])


def portable(
    tokens,
    x_weight,
    bc_weight,
    dt_weight,
    conv_x,
    conv_bc,
    dt_bias,
    decay_rate,
    d_skip,
    norm_gain,
    initial_state,
    steer,
):
    features = lax.all_gather(tokens, "tp", axis=1, tiled=True)
    rim_rows = conv_x.shape[0] - 1
    local_tokens = features.shape[0]
    head_count = dt_weight.shape[1]
    channels = x_weight.shape[1]
    head_size = channels // head_count
    bc_panel = lax.all_gather(bc_weight, "tp", axis=1, tiled=True)
    previous = passed_along(features[local_tokens - rim_rows :], "seq", 1)
    source = jnp.concatenate([previous, features], 0)
    x_sums = jnp.dot(
        source,
        lax.all_gather(x_weight, "seq", axis=0, tiled=True),
        preferred_element_type=jnp.float32,
    )
    bc_sums = jnp.dot(
        source,
        lax.all_gather(bc_panel, "seq", axis=0, tiled=True),
        preferred_element_type=jnp.float32,
    )
    dt_sums = jnp.dot(
        source,
        lax.all_gather(dt_weight, "seq", axis=0, tiled=True),
        preferred_element_type=jnp.float32,
    )
    x_pre = x_sums.astype(jnp.bfloat16)
    bc_pre = bc_sums.astype(jnp.bfloat16)
    dt_raw = dt_sums[rim_rows:]
    x_conv = convolve(x_pre, conv_x)
    bc_conv = convolve(bc_pre, conv_bc)
    b_values = bc_conv[:, :N]
    c_values = bc_conv[:, N:]
    step_size = jax.nn.softplus(dt_raw + dt_bias[None, :])
    log_decay = -step_size * decay_rate[None, :]
    blocks = local_tokens // GROUP
    x_heads = x_conv.reshape(local_tokens, head_count, head_size)
    inputs = (
        x_heads.reshape(blocks, GROUP, head_count, head_size),
        b_values.reshape(blocks, GROUP, N),
        c_values.reshape(blocks, GROUP, N),
        log_decay.reshape(blocks, GROUP, head_count),
        step_size.reshape(blocks, GROUP, head_count),
    )
    zero_state = jnp.zeros((head_count, head_size, N), jnp.float32)
    local_state, local_out = lax.scan(block_update, zero_state, inputs)
    running = jnp.cumsum(log_decay, axis=0)
    local_decay = jnp.exp(running[-1])
    identity = (
        jnp.ones((head_count,), jnp.float32),
        jnp.zeros((head_count, head_size, N), jnp.float32),
    )
    prefix_decay, prefix_state = prefix((local_decay, local_state), "seq", combine_carry, identity)
    entering = prefix_decay[:, None, None] * initial_state + prefix_state
    from_entering = jnp.einsum(
        "tn,hpn->thp", c_values.astype(jnp.float32), entering, precision=lax.Precision.HIGHEST
    )
    outputs = (
        local_out.reshape(local_tokens, head_count, head_size)
        + jnp.exp(running)[:, :, None] * from_entering
        + d_skip[None, :, None] * x_heads.astype(jnp.float32)
    )
    mean_square = jnp.mean(outputs * outputs, axis=-1, keepdims=True)
    normed = (outputs * lax.rsqrt(mean_square + EPSILON)).reshape(
        local_tokens, channels
    ) * norm_gain[None, :]
    partial_dot = jnp.sum(normed * steer[None, :], axis=1)
    total_dot = lax.psum(partial_dot, "tp")
    penalty = total_dot / jnp.sqrt(jnp.float32(channels * lax.axis_size("tp")))
    return (normed - penalty[:, None] * steer[None, :]).astype(jnp.bfloat16)


def dot(a, b):
    return jnp.dot(a, b, preferred_element_type=F32)


def split_dot(a, b):
    high = b.astype(BF16)
    low = (b - high.astype(F32)).astype(BF16)
    return dot(a, high) + dot(a, low)


def smooth(ref, at, taps):
    rows = ref[pl.ds(pl.multiple_of(at * GROUP + TAIL - 8, 8), GROUP + 8), :]
    width = taps.shape[0]
    summed = taps[0:1, :] * rows[9 - width : 9 - width + GROUP]
    for k in range(1, width):
        summed = summed + taps[k : k + 1, :] * rows[9 - width + k : 9 - width + k + GROUP]
    return (summed / (1.0 + jnp.exp(-summed))).astype(BF16)


def spread(values, heads, size):
    head = lax.broadcasted_iota(jnp.int32, (128, heads * size), 0)
    lane = lax.broadcasted_iota(jnp.int32, (128, heads * size), 1)
    chosen = (head == lane // size).astype(BF16)
    high = values.astype(BF16)
    low = (values - high.astype(F32)).astype(BF16)
    return dot(high, chosen) + dot(low, chosen)


def layer_kernel(
    planes, heads, tok_ref, xw_ref, bcw_hbm, dtw_hbm, taps_x_hbm, taps_bc_hbm, bias_hbm, rate_hbm, skip_hbm, gain_hbm, first_hbm, steer_hbm, out_ref,
    bcw, dtw, pack_ref, taps_x, taps_bc, small_in, small, gain, first, steer, load_sem,
    toks, weights, thin, wide, narrow, x_tail, x_last, bc_own, bc_all, bc_tail,
    x_pad, bc_pad, x_conv, bc_conv, s_keep, dt_keep, states, logs, y_keep, state_out, total_out, state_in, total_in,
    normed, partial, normed_in, partial_in,
    send_sem, tok_sem, sib_sem, swap_sem, line_sem, own_sem, tail_sem, bct_sem, bc_sem, state_sem, total_sem, normed_sem, partial_sem,
):
    seq, core = lax.axis_index("seq"), lax.axis_index("tp")
    plane, member = lax.div(seq, PLANE), lax.rem(seq, PLANE)
    base = plane * PLANE
    own_rows, columns = tok_ref.shape
    rows = own_rows * PLANE
    half = own_rows // 2
    depth = xw_ref.shape[0]
    channels = weights.shape[3]
    size = channels // heads
    quarter = weights.shape[2] - depth - TAIL
    blocks = rows // GROUP
    per_member = blocks // PLANE
    my_x, my_y = lax.rem(member, 2), lax.div(member, 2)

    def member_at(j):
        return lax.rem(my_y + j // 2, 2) * 2 + lax.rem(my_x + j % 2, 2)

    members = [member_at(j) for j in range(PLANE)]
    far = [lax.rem(plane + j, planes) for j in range(planes)]
    has_below, has_above = plane > 0, plane < planes - 1

    loads = [
        (bcw_hbm, bcw), (dtw_hbm, dtw), (taps_x_hbm, taps_x), (taps_bc_hbm, taps_bc), (bias_hbm, small_in.at[0]),
        (rate_hbm, small_in.at[1]), (skip_hbm, small_in.at[2]), (gain_hbm, gain), (steer_hbm, steer),
        (first_hbm.at[pl.ds(pl.multiple_of(member * channels, channels), channels)], first),
    ]
    loads = [pltpu.make_async_copy(source, target, load_sem.at[i]) for i, (source, target) in enumerate(loads)]
    for copy in loads:
        copy.start()
    barrier = pltpu.get_barrier_semaphore()

    def greet(s, c):
        pl.semaphore_signal(barrier, inc=1, device_id=(s, c), device_id_type=MESH)

    for j in range(PLANE):
        greet(base + members[j], 1 - core)
        if j:
            greet(base + members[j], core)

    @pl.when(has_below)
    def _():
        for m in range(PLANE):
            for c in range(2):
                greet(base - PLANE + m, c)

    @pl.when(has_above)
    def _():
        for m in range(PLANE):
            for c in range(2):
                greet(base + PLANE + m, c)

    greeted = 2 * PLANE - 1 + jnp.where(has_below, 2 * PLANE, 0) + jnp.where(has_above, 2 * PLANE, 0)
    for j in range(1, planes):
        distant = jnp.abs(far[j] - plane) > 1
        pl.when(distant)(lambda j=j: greet(far[j] * PLANE + member, core))
        greeted = greeted + jnp.where(distant, 1, 0)
    pl.semaphore_wait(barrier, greeted)

    started = []

    def send(source, target, sem, device, when=None):
        copy = pltpu.make_async_remote_copy(
            src_ref=source, dst_ref=target, send_sem=send_sem.at[len(started)], recv_sem=sem,
            device_id=device, device_id_type=MESH,
        )
        started.append((copy, when))
        if when is None:
            copy.start()
        else:
            pl.when(when)(lambda: copy.start())

    def arrived(target, sem, when=None):
        copy = pltpu.make_async_remote_copy(
            src_ref=target, dst_ref=target, send_sem=send_sem.at[0], recv_sem=sem,
            device_id=(seq, 1 - core), device_id_type=MESH,
        )
        if when is None:
            copy.wait_recv()
        else:
            pl.when(when)(lambda: copy.wait_recv())

    def piece(c, j, h):
        return toks.at[c, pl.ds(pl.multiple_of(members[j] * own_rows + h * half, half), half)]

    def own_piece(h):
        return tok_ref.at[pl.ds(h * half, half)]

    def block(p, j):
        return weights.at[p, members[j]]

    across = [(base + members[j], core) for j in range(PLANE)]
    up, down, sibling = (seq + PLANE, core), (seq - PLANE, core), (seq, 1 - core)

    def quarter_of(m):
        return xw_ref.at[:, pl.ds(pl.multiple_of(m * channels, channels), channels)]

    def wide_part(m, *where):
        send(quarter_of(m), weights.at[plane, member, pl.ds(0, depth)], *where)

    def thin_part(m, *where):
        send(pack_ref.at[m], weights.at[plane, member, pl.ds(depth, quarter + TAIL)], *where)

    own_copies = [
        pltpu.make_async_copy(quarter_of(member), weights.at[plane, member, pl.ds(0, depth)], own_sem.at[0]),
        pltpu.make_async_copy(pack_ref.at[member], weights.at[plane, member, pl.ds(depth, quarter + TAIL)], own_sem.at[1]),
        pltpu.make_async_copy(tok_ref, toks.at[core, pl.ds(pl.multiple_of(member * own_rows, own_rows), own_rows)], own_sem.at[2]),
    ]
    own_copies[0].start()
    own_copies[2].start()

    def first_parts(part):
        for j in (1, 2, 3):
            part(members[j], swap_sem.at[j], across[j])
        part(member, line_sem.at[0, 1, 0], up, has_above)
        part(member, line_sem.at[1, 1, 0], down, has_below)

    first_parts(wide_part)
    loads[0].wait()
    loads[1].wait()
    turned = bcw[...].astype(F32).T.astype(BF16)
    for m in range(PLANE):
        pack_ref[m, 0:quarter, :] = turned[m * quarter : (m + 1) * quarter]
        pack_ref[m, quarter:, :] = dtw[...]
    own_copies[1].start()
    first_parts(thin_part)
    send(own_piece(0), piece(core, 0, 0), tok_sem.at[0], across[1])
    send(own_piece(1), piece(core, 0, 1), tok_sem.at[2], across[2])
    send(own_piece(1), piece(core, 0, 1), tok_sem.at[1], across[1])
    send(own_piece(0), piece(core, 0, 0), tok_sem.at[3], across[2])
    send(own_piece(0), piece(core, 0, 0), sib_sem.at[0, 0], sibling)
    send(own_piece(1), piece(core, 0, 1), sib_sem.at[0, 1], sibling)
    for j in (1, 2, 3):
        arrived(block(plane, j), swap_sem.at[j])
        send(block(plane, j), block(plane, j), line_sem.at[0, 1, j], up, has_above)
        send(block(plane, j), block(plane, j), line_sem.at[1, 1, j], down, has_below)

    def relay(step, j):
        lower, upper = plane - step, plane + step
        arrived(block(jnp.maximum(lower, 0), j), line_sem.at[0, step, j], lower >= 0)
        arrived(block(jnp.minimum(upper, planes - 1), j), line_sem.at[1, step, j], upper < planes)
        if step < planes - 1:
            low = block(jnp.maximum(lower, 0), j)
            high = block(jnp.minimum(upper, planes - 1), j)
            send(low, low, line_sem.at[0, step + 1, j], up, jnp.logical_and(lower >= 0, has_above))
            send(high, high, line_sem.at[1, step + 1, j], down, jnp.logical_and(upper < planes, has_below))

    def token(j, h, index, forward=None):
        here = piece(core, j, h)
        arrived(here, tok_sem.at[index])
        if forward is not None:
            send(here, here, tok_sem.at[forward[0]], across[forward[1]])
        send(here, here, sib_sem.at[j, h], sibling)

    def from_sibling(j):
        for h in range(2):
            arrived(piece(1 - core, j, h), sib_sem.at[j, h])

    filler = jnp.zeros((128 - quarter - TAIL, depth), F32)

    def turn(lowest, highest):
        def one(p, _):
            for k in range(PLANE):
                block_rows = jnp.concatenate([weights[p, k, depth:, :].astype(F32), filler], 0)
                thin[p * PLANE + k] = block_rows.T.astype(BF16)
            return 0

        lax.fori_loop(lowest, highest, one, 0)

    def multiply(j, p):
        where = pl.ds(pl.multiple_of(member_at(j) * own_rows, own_rows), own_rows)
        per_core = columns // (PLANE * depth)
        side = p // per_core
        total_wide, total_narrow = wide[where, :], narrow[where, :]
        for k in range(PLANE):
            span = pl.ds(pl.multiple_of((p % per_core) * (PLANE * depth) + k * depth, depth), depth)
            left = toks[side, where, span]
            total_wide += dot(left, weights[p, k, 0:depth, :])
            total_narrow += dot(left, thin[p * PLANE + k])
        wide[where, :] = total_wide
        narrow[where, :] = total_narrow

    def multiply_all(parts, lowest, highest):
        first_part, last_part = parts

        def at(j, _):
            return lax.fori_loop(lowest, highest, lambda p, _: (multiply(j, p), 0)[1], 0)

        lax.fori_loop(first_part, last_part, at, 0)

    wide[...] = jnp.zeros_like(wide)
    narrow[...] = jnp.zeros_like(narrow)
    takes = [
        (1, 0, 0, (4, 2)), (2, 1, 2, (5, 1)), (1, 1, 1, None), (2, 0, 3, None),
    ]
    places = [3, 3, 6, 6]
    near_low, near_high = jnp.maximum(plane - (planes - 2), 0), jnp.minimum(plane + planes - 1, planes)
    steps = [(step, j) for step in range(1, planes) for j in range(PLANE)]
    for at, (step, j) in enumerate(steps):
        for take, place in zip(takes, places):
            if min(place, len(steps) - 1) == at:
                token(*take)
        if at == len(steps) - PLANE + 1:
            for copy in own_copies:
                copy.wait()
            for i in range(3):
                from_sibling(i)
            turn(near_low, near_high)
            multiply_all((0, 3), near_low, near_high)
            token(3, 0, 4)
        if at == len(steps) - 1:
            token(3, 1, 5)
        relay(step, j)
    turn(0, near_low)
    turn(near_high, planes)
    multiply_all((0, 3), 0, near_low)
    multiply_all((0, 3), near_high, planes)
    from_sibling(3)
    multiply_all((3, 4), 0, planes)

    x_last[...] = wide[rows - TAIL : rows, :].astype(BF16)
    send(x_last, x_tail, tail_sem, up, has_above)
    me = core * PLANE + member
    for i in range(PLANE):
        part = rows // PLANE
        bc_own[:, i * part : (i + 1) * part] = narrow[i * part : (i + 1) * part, :].T[0:quarter, :].astype(BF16)
    for j in (3, 1, 2):
        send(bc_own, bc_all.at[me], bc_sem.at[me], across[j])
    send(bc_own, bc_all.at[me], bc_sem.at[me], sibling)
    last = bc_own.at[:, pl.ds(rows - GROUP, GROUP)]
    for m in range(PLANE):
        for c in range(2):
            send(last, bc_tail.at[me], bct_sem.at[me], (base + PLANE + m, c), has_above)
    bc_all[me] = bc_own[...]

    mine = pl.ds(pl.multiple_of(member * channels, channels), channels)
    for copy in loads[2:]:
        copy.wait()
    small[...] = jnp.zeros_like(small)
    for i in range(3):
        small[i : i + 1, 0 : PLANE * heads] = small_in[i]
    own_small = pltpu.roll(small[...], lax.rem(128 - member * heads, 128), 1)
    bias, rate = own_small[0:1, :], own_small[1:2, :]
    skip = spread(own_small, heads, size)[2:3, :]
    taps = taps_x[:, mine]
    own_gain, own_steer = gain[:, mine], steer[:, mine]
    row = lax.broadcasted_iota(jnp.int32, (GROUP, GROUP), 0)
    column = lax.broadcasted_iota(jnp.int32, (GROUP, GROUP), 1)
    causal = row >= column
    lower = causal.astype(BF16)

    def here(at):
        return pl.ds(pl.multiple_of(at * GROUP, GROUP), GROUP)

    def steps_of(at, _):
        raw = pltpu.roll(narrow[here(at), :], 128 - quarter - member * heads, 1) + bias
        dt = jnp.maximum(raw, 0.0) + jnp.log1p(jnp.exp(-jnp.abs(raw)))
        a = -dt * rate
        one = a.astype(BF16)
        rest = a - one.astype(F32)
        two = rest.astype(BF16)
        three = (rest - two.astype(F32)).astype(BF16)
        s_keep[here(at), :] = dot(lower, one) + (dot(lower, two) + dot(lower, three))
        dt_keep[here(at), :] = dt
        x_pad[pl.ds(pl.multiple_of(at * GROUP + TAIL, TAIL), GROUP), :] = wide[here(at), :].astype(BF16).astype(F32)
        return 0

    lax.fori_loop(0, blocks, steps_of, 0, unroll=4)
    for j in (1, 2, 3):
        slot = core * PLANE + members[j]
        arrived(bc_all.at[slot], bc_sem.at[slot])
        send(bc_all.at[slot], bc_all.at[slot], bc_sem.at[slot], sibling)

    @pl.when(jnp.logical_not(has_below))
    def _():
        x_tail[...] = jnp.zeros_like(x_tail)
        bc_tail[...] = jnp.zeros_like(bc_tail)

    arrived(x_tail, tail_sem, has_below)
    x_pad[0:TAIL, :] = x_tail[...].astype(F32)

    def convolved(at, _):
        x_conv[here(at), :] = smooth(x_pad, at, taps)
        return 0

    lax.fori_loop(0, blocks, convolved, 0, unroll=4)

    for j in range(PLANE):
        slot = (1 - core) * PLANE + members[j]
        arrived(bc_all.at[slot], bc_sem.at[slot])
    for sender in range(2 * PLANE):
        arrived(bc_tail.at[sender], bct_sem.at[sender], has_below)
    bc_pad[0:TAIL, :] = bc_tail[...].astype(F32).reshape(2 * N, GROUP).T[GROUP - TAIL :, :]

    def unturned(at, _):
        turned = bc_all[:, :, here(at)].astype(F32).reshape(2 * N, GROUP)
        bc_pad[pl.ds(pl.multiple_of(at * GROUP + TAIL, TAIL), GROUP), :] = turned.T
        return 0

    lax.fori_loop(0, blocks, unturned, 0, unroll=4)

    def advance(at, carry):
        state, log = carry
        bc = smooth(bc_pad, at, taps_bc[...])
        bc_conv[here(at), :] = bc
        s = s_keep[here(at), :]
        states[at] = state
        logs[at] = log
        end = s[GROUP - 1 : GROUP, :]
        weight = spread(jnp.exp(end - s) * dt_keep[here(at), :], heads, size)
        scaled = (x_conv[here(at), :].astype(F32) * weight).astype(BF16)
        b_turned = bc[:, :N].astype(F32).T.astype(BF16)
        ended = jnp.broadcast_to(end, (8, 128))
        state = spread(jnp.exp(ended), heads, size)[0:1, :] * state + dot(b_turned, scaled)
        return state, log + ended

    zeros = (jnp.zeros((N, channels), F32), jnp.zeros((8, 128), F32))
    state, log = lax.fori_loop(0, blocks, advance, zeros, unroll=4)
    state_out[...] = state.astype(BF16)
    total_out[...] = log
    for j in range(1, planes):
        other = (far[j] * PLANE + member, core)
        send(state_out, state_in.at[planes - j], state_sem.at[planes - j], other)
        send(total_out, total_in.at[planes - j], total_sem.at[planes - j], other)

    def inside(at, _):
        x = x_conv[here(at), :]
        bc = bc_conv[here(at), :]
        s = s_keep[here(at), :]
        s_turned = s.T
        dt_turned = dt_keep[here(at), :].T
        scores = lax.dot_general(bc[:, N:], bc[:, :N], (((1,), (1,)), ((), ())), preferred_element_type=F32)
        parts = []
        for h in range(heads):
            differ = s[:, h : h + 1] - s_turned[h : h + 1, :]
            decays = jnp.where(causal, jnp.exp(jnp.where(causal, differ, 0.0)), 0.0)
            mixing = (scores * decays * dt_turned[h : h + 1, :]).astype(BF16)
            parts.append(dot(mixing, x[:, h * size : (h + 1) * size]))
        y_keep[here(at), :] = jnp.concatenate(parts, 1) + skip * x.astype(F32)
        return 0

    lax.fori_loop(0, blocks, inside, 0, unroll=4)

    entering = first[...].T
    for j in range(1, planes):
        arrived(state_in.at[j], state_sem.at[j])
        arrived(total_in.at[j], total_sem.at[j])
    for j in range(1, planes):
        later = spread(jnp.exp(total_in[j]), heads, size)[0:1, :] * entering + state_in[j].astype(F32)
        entering = jnp.where(far[j] < plane, later, entering)

    group_of = lax.broadcasted_iota(jnp.int32, (2, channels, channels), 1) // size
    same = (group_of[0] == lax.broadcasted_iota(jnp.int32, (channels, channels), 1) // size).astype(BF16)

    def finish(at):
        s = s_keep[here(at), :]
        c = bc_conv[here(at), :][:, N:]
        state = states[at] + spread(jnp.exp(logs[at]), heads, size)[0:1, :] * entering
        y = y_keep[here(at), :] + spread(jnp.exp(s), heads, size) * split_dot(c, state)
        square = y * y
        high = square.astype(BF16)
        low = (square - high.astype(F32)).astype(BF16)
        mean = (dot(high, same) + dot(low, same)) * (1.0 / size)
        scaled = y * lax.rsqrt(mean + EPSILON) * own_gain
        normed[here(at), :] = scaled.astype(BF16)
        along = jnp.sum(scaled * own_steer, axis=1, keepdims=True)
        partial[at] = jnp.broadcast_to(along, (GROUP, GROUP)).T[0:8, :]

    for j in (3, 1, 2, 0):
        target = members[j]
        lax.fori_loop(0, per_member, lambda i, _: (finish(target * per_member + i), 0)[1], 0, unroll=2)
        pieces = partial.at[pl.ds(target * per_member, per_member)]
        if j:
            chunk = normed.at[pl.ds(pl.multiple_of(target * own_rows, own_rows), own_rows)]
            send(chunk, normed_in.at[member], normed_sem.at[j], (base + target, core))
            send(pieces, partial_in.at[0, j], partial_sem.at[0, j], (base + target, core))
        send(pieces, partial_in.at[1, j], partial_sem.at[1, j], (base + target, 1 - core))
    normed_in[member] = normed[pl.ds(pl.multiple_of(member * own_rows, own_rows), own_rows), :]
    penalty = partial[pl.ds(member * per_member, per_member)]
    for j in range(PLANE):
        if j:
            arrived(normed_in.at[members[j]], normed_sem.at[j])
            arrived(partial_in.at[0, j], partial_sem.at[0, j])
            penalty = penalty + partial_in[0, j]
        arrived(partial_in.at[1, j], partial_sem.at[1, j])
        penalty = penalty + partial_in[1, j]
    penalty = penalty * (1.0 / (channels * PLANE * lax.axis_size("tp")) ** 0.5)
    for i in range(per_member):
        turned = jnp.broadcast_to(penalty[i][0:1, :], (GROUP, GROUP)).T
        turned = jnp.concatenate([turned] * (channels // GROUP), 1)
        span = pl.ds(i * GROUP, GROUP)
        for j in range(PLANE):
            value = normed_in[j, span, :].astype(F32) - turned * steer[:, j * channels : (j + 1) * channels]
            out_ref[span, j * channels : (j + 1) * channels] = value.astype(BF16)
    for copy, when in started:
        if when is None:
            copy.wait_send()
        else:
            pl.when(when)(lambda copy=copy: copy.wait_send())


def per_device(tokens, x_weight, bc_weight, dt_weight, conv_x, conv_bc, dt_bias, decay_rate, d_skip, norm_gain, initial_state, steer):
    planes = lax.axis_size("seq") // PLANE
    own_rows, columns = tokens.shape
    depth, all_channels = x_weight.shape
    all_heads = dt_weight.shape[1]
    channels, heads = all_channels // PLANE, all_heads // PLANE
    rows = own_rows * PLANE
    blocks = rows // GROUP
    quarter = bc_weight.shape[1] // PLANE

    vmem = pl.BlockSpec(memory_space=pltpu.VMEM)
    far = pl.BlockSpec(memory_space=pltpu.HBM)
    dma = pltpu.SemaphoreType.DMA
    out = pl.pallas_call(
        functools.partial(layer_kernel, planes, heads),
        out_shape=jax.ShapeDtypeStruct((own_rows, all_channels), BF16),
        in_specs=[far] * 12,
        out_specs=vmem,
        scratch_shapes=[
            pltpu.VMEM(bc_weight.shape, BF16),
            pltpu.VMEM((all_heads, depth), BF16),
            pltpu.VMEM((PLANE, quarter + TAIL, depth), BF16),
            pltpu.VMEM(conv_x.shape, F32),
            pltpu.VMEM(conv_bc.shape, F32),
            pltpu.VMEM((3, 1, all_heads), F32),
            pltpu.VMEM((8, 128), F32),
            pltpu.VMEM((1, all_channels), F32),
            pltpu.VMEM((channels, N), F32),
            pltpu.VMEM((1, all_channels), F32),
            dma((10,)),
            pltpu.VMEM((2, rows, columns), BF16),
            pltpu.VMEM((planes, PLANE, depth + quarter + TAIL, channels), BF16),
            pltpu.VMEM((planes * PLANE, depth, 128), BF16),
            pltpu.VMEM((rows, channels), F32),
            pltpu.VMEM((rows, 128), F32),
            pltpu.VMEM((TAIL, channels), BF16),
            pltpu.VMEM((TAIL, channels), BF16),
            pltpu.VMEM((quarter, rows), BF16),
            pltpu.VMEM((2 * PLANE, quarter, rows), BF16),
            pltpu.VMEM((2 * PLANE, quarter, GROUP), BF16),
            pltpu.VMEM((rows + TAIL, channels), F32),
            pltpu.VMEM((rows + TAIL, 2 * N), F32),
            pltpu.VMEM((rows, channels), BF16),
            pltpu.VMEM((rows, 2 * N), BF16),
            pltpu.VMEM((rows, 128), F32),
            pltpu.VMEM((rows, 128), F32),
            pltpu.VMEM((blocks, N, channels), F32),
            pltpu.VMEM((blocks, 8, 128), F32),
            pltpu.VMEM((rows, channels), F32),
            pltpu.VMEM((N, channels), BF16),
            pltpu.VMEM((8, 128), F32),
            pltpu.VMEM((planes, N, channels), BF16),
            pltpu.VMEM((planes, 8, 128), F32),
            pltpu.VMEM((rows, channels), BF16),
            pltpu.VMEM((blocks, 8, GROUP), F32),
            pltpu.VMEM((PLANE, own_rows, channels), BF16),
            pltpu.VMEM((2, PLANE, blocks // PLANE, 8, GROUP), F32),
            dma((64 + 10 * planes,)),
            dma((6,)),
            dma((PLANE, 2)),
            dma((PLANE,)),
            dma((2, planes, PLANE)),
            dma((3,)),
            dma(()),
            dma((2 * PLANE,)),
            dma((2 * PLANE,)),
            dma((planes,)),
            dma((planes,)),
            dma((PLANE,)),
            dma((2, PLANE)),
        ],
        compiler_params=pltpu.CompilerParams(collective_id=0, has_side_effects=True, vmem_limit_bytes=60 * 2**20),
    )(
        tokens, x_weight, bc_weight, dt_weight.T, conv_x, conv_bc, dt_bias[None, :], decay_rate[None, :], d_skip[None, :],
        norm_gain[None, :], initial_state.reshape(all_channels, N), steer[None, :],
    )
    return out


def solution(mesh):
    placed = (
        P("seq", "tp"),
        P("seq", "tp"),
        P("seq", "tp"),
        P("seq", "tp"),
        P(None, "tp"),
        P(),
        P("tp"),
        P("tp"),
        P("tp"),
        P("tp"),
        P("tp", None, None),
        P("tp"),
    )
    planar = mesh.shape["tp"] == 2 and mesh.shape["seq"] % PLANE == 0
    return jax.shard_map(
        per_device if planar else portable, mesh=mesh, in_specs=placed, out_specs=P("seq", "tp"), check_vma=False
    )
```

```python
import functools

import jax
import jax.numpy as jnp
from jax import lax
from jax.experimental import pallas as pl
from jax.experimental.pallas import tpu as pltpu
from jax.sharding import PartitionSpec as P

MESH = pl.DeviceIdType.MESH
PLANE = 4
TAIL = 16
F32 = jnp.float32
BF16 = jnp.bfloat16

N = 128
GROUP = 128


EPSILON = 1e-05


def passed_along(value, axis, steps):
    count = lax.axis_size(axis)
    first, last = (max(0, -steps), min(count, count - steps))
    return lax.ppermute(value, axis, [(source, source + steps) for source in range(first, last)])


def prefix(x, axis, combine, identity):
    count, mine = (lax.axis_size(axis), lax.axis_index(axis))
    everything = jax.tree.map(
        lambda part, kind: lax.all_gather(part.astype(kind), axis), x, (jnp.bfloat16, jnp.bfloat16)
    )
    start = jax.tree.map(
        lambda part, zero: jnp.broadcast_to(jnp.asarray(zero, part.dtype), part.shape), x, identity
    )

    def turn(k, before):
        reached = k < mine
        new = combine(
            before, jax.tree.map(lambda part, own: part[k].astype(own.dtype), everything, x)
        )
        return jax.tree.map(lambda a, b: jnp.where(reached, a, b), new, before)

    return lax.fori_loop(0, count, turn, start)


def convolve(extended, kernel):
    kernel_rows = kernel.shape[0]
    length = extended.shape[0] - kernel_rows + 1
    summed = kernel[0] * extended[0:length].astype(jnp.float32)
    for offset in range(1, kernel_rows):
        summed = summed + kernel[offset] * extended[offset : offset + length].astype(jnp.float32)
    return jax.nn.silu(summed).astype(jnp.bfloat16)


def block_update(carry_state, inputs):
    x_block, b_block, c_block, a_block, dt_block = inputs
    length = a_block.shape[0]
    cumulative = jnp.cumsum(a_block, axis=0)
    scores = jnp.dot(c_block, b_block.T, preferred_element_type=jnp.float32)
    causal = lax.broadcasted_iota(jnp.int32, (length, length), 0) >= lax.broadcasted_iota(
        jnp.int32, (length, length), 1
    )
    differ = cumulative[:, None, :] - cumulative[None, :, :]
    decays = jnp.where(causal[:, :, None], jnp.exp(jnp.where(causal[:, :, None], differ, 0.0)), 0.0)
    mixing = (scores[:, :, None] * decays * dt_block[None, :, :]).astype(jnp.bfloat16)
    inside = jnp.einsum("tsh,shp->thp", mixing, x_block, preferred_element_type=jnp.float32)
    carried_in = jnp.einsum(
        "tn,hpn->thp", c_block.astype(jnp.float32), carry_state, precision=lax.Precision.HIGHEST
    )
    outputs = inside + jnp.exp(cumulative)[:, :, None] * carried_in
    to_end = jnp.exp(cumulative[-1][None, :] - cumulative) * dt_block
    scaled = (x_block.astype(jnp.float32) * to_end[:, :, None]).astype(jnp.bfloat16)
    added_state = jnp.einsum("shp,sn->hpn", scaled, b_block, preferred_element_type=jnp.float32)
    return (jnp.exp(cumulative[-1])[:, None, None] * carry_state + added_state, outputs)


def combine_carry(earlier, later):
    return (earlier[0] * later[0], later[0][:, None, None] * earlier[1] + later[1])


def portable(
    tokens,
    x_weight,
    bc_weight,
    dt_weight,
    conv_x,
    conv_bc,
    dt_bias,
    decay_rate,
    d_skip,
    norm_gain,
    initial_state,
    steer,
):
    features = lax.all_gather(tokens, "tp", axis=1, tiled=True)
    rim_rows = conv_x.shape[0] - 1
    local_tokens = features.shape[0]
    head_count = dt_weight.shape[1]
    channels = x_weight.shape[1]
    head_size = channels // head_count
    bc_panel = lax.all_gather(bc_weight, "tp", axis=1, tiled=True)
    previous = passed_along(features[local_tokens - rim_rows :], "seq", 1)
    source = jnp.concatenate([previous, features], 0)
    x_sums = jnp.dot(
        source,
        lax.all_gather(x_weight, "seq", axis=0, tiled=True),
        preferred_element_type=jnp.float32,
    )
    bc_sums = jnp.dot(
        source,
        lax.all_gather(bc_panel, "seq", axis=0, tiled=True),
        preferred_element_type=jnp.float32,
    )
    dt_sums = jnp.dot(
        source,
        lax.all_gather(dt_weight, "seq", axis=0, tiled=True),
        preferred_element_type=jnp.float32,
    )
    x_pre = x_sums.astype(jnp.bfloat16)
    bc_pre = bc_sums.astype(jnp.bfloat16)
    dt_raw = dt_sums[rim_rows:]
    x_conv = convolve(x_pre, conv_x)
    bc_conv = convolve(bc_pre, conv_bc)
    b_values = bc_conv[:, :N]
    c_values = bc_conv[:, N:]
    step_size = jax.nn.softplus(dt_raw + dt_bias[None, :])
    log_decay = -step_size * decay_rate[None, :]
    blocks = local_tokens // GROUP
    x_heads = x_conv.reshape(local_tokens, head_count, head_size)
    inputs = (
        x_heads.reshape(blocks, GROUP, head_count, head_size),
        b_values.reshape(blocks, GROUP, N),
        c_values.reshape(blocks, GROUP, N),
        log_decay.reshape(blocks, GROUP, head_count),
        step_size.reshape(blocks, GROUP, head_count),
    )
    zero_state = jnp.zeros((head_count, head_size, N), jnp.float32)
    local_state, local_out = lax.scan(block_update, zero_state, inputs)
    running = jnp.cumsum(log_decay, axis=0)
    local_decay = jnp.exp(running[-1])
    identity = (
        jnp.ones((head_count,), jnp.float32),
        jnp.zeros((head_count, head_size, N), jnp.float32),
    )
    prefix_decay, prefix_state = prefix((local_decay, local_state), "seq", combine_carry, identity)
    entering = prefix_decay[:, None, None] * initial_state + prefix_state
    from_entering = jnp.einsum(
        "tn,hpn->thp", c_values.astype(jnp.float32), entering, precision=lax.Precision.HIGHEST
    )
    outputs = (
        local_out.reshape(local_tokens, head_count, head_size)
        + jnp.exp(running)[:, :, None] * from_entering
        + d_skip[None, :, None] * x_heads.astype(jnp.float32)
    )
    mean_square = jnp.mean(outputs * outputs, axis=-1, keepdims=True)
    normed = (outputs * lax.rsqrt(mean_square + EPSILON)).reshape(
        local_tokens, channels
    ) * norm_gain[None, :]
    partial_dot = jnp.sum(normed * steer[None, :], axis=1)
    total_dot = lax.psum(partial_dot, "tp")
    penalty = total_dot / jnp.sqrt(jnp.float32(channels * lax.axis_size("tp")))
    return (normed - penalty[:, None] * steer[None, :]).astype(jnp.bfloat16)


def dot(a, b):
    return jnp.dot(a, b, preferred_element_type=F32)


def split_dot(a, b):
    high = b.astype(BF16)
    low = (b - high.astype(F32)).astype(BF16)
    return dot(a, high) + dot(a, low)


def smooth(ref, at, taps):
    rows = ref[pl.ds(pl.multiple_of(at * GROUP + TAIL - 8, 8), GROUP + 8), :]
    width = taps.shape[0]
    summed = taps[0:1, :] * rows[9 - width : 9 - width + GROUP]
    for k in range(1, width):
        summed = summed + taps[k : k + 1, :] * rows[9 - width + k : 9 - width + k + GROUP]
    return (summed / (1.0 + jnp.exp(-summed))).astype(BF16)


def spread(values, heads, size):
    head = lax.broadcasted_iota(jnp.int32, (128, heads * size), 0)
    lane = lax.broadcasted_iota(jnp.int32, (128, heads * size), 1)
    chosen = (head == lane // size).astype(BF16)
    high = values.astype(BF16)
    low = (values - high.astype(F32)).astype(BF16)
    return dot(high, chosen) + dot(low, chosen)


def layer_kernel(
    planes, heads, tok_ref, xw_ref, bcw_hbm, dtw_hbm, taps_x_hbm, taps_bc_hbm, bias_hbm, rate_hbm, skip_hbm, gain_hbm, first_hbm, steer_hbm, out_ref,
    bcw, dtw, pack_ref, taps_x, taps_bc, small_in, small, gain, first, steer, load_sem,
    toks, weights, thin, wide, narrow, x_tail, x_last, bc_own, bc_all, bc_tail,
    x_pad, bc_pad, x_conv, bc_conv, s_keep, dt_keep, states, logs, y_keep, state_out, total_out, state_in, total_in,
    normed, partial, normed_in, partial_in,
    send_sem, tok_sem, sib_sem, swap_sem, line_sem, own_sem, tail_sem, bct_sem, bc_sem, state_sem, total_sem, normed_sem, partial_sem,
):
    seq, core = lax.axis_index("seq"), lax.axis_index("tp")
    plane, member = lax.div(seq, PLANE), lax.rem(seq, PLANE)
    base = plane * PLANE
    own_rows, columns = tok_ref.shape
    rows = own_rows * PLANE
    half = own_rows // 2
    depth = xw_ref.shape[0]
    channels = weights.shape[3]
    size = channels // heads
    quarter = weights.shape[2] - depth - TAIL
    blocks = rows // GROUP
    per_member = blocks // PLANE
    my_x, my_y = lax.rem(member, 2), lax.div(member, 2)

    def member_at(j):
        return lax.rem(my_y + j // 2, 2) * 2 + lax.rem(my_x + j % 2, 2)

    members = [member_at(j) for j in range(PLANE)]
    far = [lax.rem(plane + j, planes) for j in range(planes)]
    has_below, has_above = plane > 0, plane < planes - 1

    loads = [
        (bcw_hbm, bcw), (dtw_hbm, dtw), (taps_x_hbm, taps_x), (taps_bc_hbm, taps_bc), (bias_hbm, small_in.at[0]),
        (rate_hbm, small_in.at[1]), (skip_hbm, small_in.at[2]), (gain_hbm, gain), (steer_hbm, steer),
        (first_hbm.at[pl.ds(pl.multiple_of(member * channels, channels), channels)], first),
    ]
    loads = [pltpu.make_async_copy(source, target, load_sem.at[i]) for i, (source, target) in enumerate(loads)]
    for copy in loads:
        copy.start()
    barrier = pltpu.get_barrier_semaphore()

    def greet(s, c):
        pl.semaphore_signal(barrier, inc=1, device_id=(s, c), device_id_type=MESH)

    for j in range(PLANE):
        greet(base + members[j], 1 - core)
        if j:
            greet(base + members[j], core)

    @pl.when(has_below)
    def _():
        for m in range(PLANE):
            for c in range(2):
                greet(base - PLANE + m, c)

    @pl.when(has_above)
    def _():
        for m in range(PLANE):
            for c in range(2):
                greet(base + PLANE + m, c)

    greeted = 2 * PLANE - 1 + jnp.where(has_below, 2 * PLANE, 0) + jnp.where(has_above, 2 * PLANE, 0)
    for j in range(1, planes):
        distant = jnp.abs(far[j] - plane) > 1
        pl.when(distant)(lambda j=j: greet(far[j] * PLANE + member, core))
        greeted = greeted + jnp.where(distant, 1, 0)
    loads[0].wait()
    loads[1].wait()
    turned = bcw[...].astype(F32).T.astype(BF16)
    for m in range(PLANE):
        pack_ref[m, 0:quarter, :] = turned[m * quarter : (m + 1) * quarter]
        pack_ref[m, quarter:, :] = dtw[...]
    pl.semaphore_wait(barrier, greeted)

    started = []

    def send(source, target, sem, device, when=None):
        copy = pltpu.make_async_remote_copy(
            src_ref=source, dst_ref=target, send_sem=send_sem.at[len(started)], recv_sem=sem,
            device_id=device, device_id_type=MESH,
        )
        started.append((copy, when))
        if when is None:
            copy.start()
        else:
            pl.when(when)(lambda: copy.start())

    def arrived(target, sem, when=None):
        copy = pltpu.make_async_remote_copy(
            src_ref=target, dst_ref=target, send_sem=send_sem.at[0], recv_sem=sem,
            device_id=(seq, 1 - core), device_id_type=MESH,
        )
        if when is None:
            copy.wait_recv()
        else:
            pl.when(when)(lambda: copy.wait_recv())

    def piece(c, j, h):
        return toks.at[c, pl.ds(pl.multiple_of(members[j] * own_rows + h * half, half), half)]

    def own_piece(h):
        return tok_ref.at[pl.ds(h * half, half)]

    def block(p, j):
        return weights.at[p, members[j]]

    across = [(base + members[j], core) for j in range(PLANE)]
    up, down, sibling = (seq + PLANE, core), (seq - PLANE, core), (seq, 1 - core)

    def quarter_of(m):
        return xw_ref.at[:, pl.ds(pl.multiple_of(m * channels, channels), channels)]

    def wide_part(m, *where):
        send(quarter_of(m), weights.at[plane, member, pl.ds(0, depth)], *where)

    def thin_part(m, *where):
        send(pack_ref.at[m], weights.at[plane, member, pl.ds(depth, quarter + TAIL)], *where)

    own_copies = [
        pltpu.make_async_copy(quarter_of(member), weights.at[plane, member, pl.ds(0, depth)], own_sem.at[0]),
        pltpu.make_async_copy(pack_ref.at[member], weights.at[plane, member, pl.ds(depth, quarter + TAIL)], own_sem.at[1]),
        pltpu.make_async_copy(tok_ref, toks.at[core, pl.ds(pl.multiple_of(member * own_rows, own_rows), own_rows)], own_sem.at[2]),
    ]
    own_copies[0].start()
    own_copies[2].start()

    def first_parts(part):
        for j in (1, 2, 3):
            part(members[j], swap_sem.at[j], across[j])
        part(member, line_sem.at[0, 1, 0], up, has_above)
        part(member, line_sem.at[1, 1, 0], down, has_below)

    first_parts(wide_part)
    own_copies[1].start()
    first_parts(thin_part)
    send(own_piece(0), piece(core, 0, 0), tok_sem.at[0], across[1])
    send(own_piece(1), piece(core, 0, 1), tok_sem.at[2], across[2])
    send(own_piece(1), piece(core, 0, 1), tok_sem.at[1], across[1])
    send(own_piece(0), piece(core, 0, 0), tok_sem.at[3], across[2])
    send(own_piece(0), piece(core, 0, 0), sib_sem.at[0, 0], sibling)
    send(own_piece(1), piece(core, 0, 1), sib_sem.at[0, 1], sibling)
    for j in (1, 2, 3):
        arrived(block(plane, j), swap_sem.at[j])
        send(block(plane, j), block(plane, j), line_sem.at[0, 1, j], up, has_above)
        send(block(plane, j), block(plane, j), line_sem.at[1, 1, j], down, has_below)

    def relay(step, j):
        lower, upper = plane - step, plane + step
        arrived(block(jnp.maximum(lower, 0), j), line_sem.at[0, step, j], lower >= 0)
        arrived(block(jnp.minimum(upper, planes - 1), j), line_sem.at[1, step, j], upper < planes)
        if step < planes - 1:
            low = block(jnp.maximum(lower, 0), j)
            high = block(jnp.minimum(upper, planes - 1), j)
            send(low, low, line_sem.at[0, step + 1, j], up, jnp.logical_and(lower >= 0, has_above))
            send(high, high, line_sem.at[1, step + 1, j], down, jnp.logical_and(upper < planes, has_below))

    def token(j, h, index, forward=None):
        here = piece(core, j, h)
        arrived(here, tok_sem.at[index])
        if forward is not None:
            send(here, here, tok_sem.at[forward[0]], across[forward[1]])
        send(here, here, sib_sem.at[j, h], sibling)

    def from_sibling(j):
        for h in range(2):
            arrived(piece(1 - core, j, h), sib_sem.at[j, h])

    filler = jnp.zeros((128 - quarter - TAIL, depth), F32)

    def turn(lowest, highest):
        def one(p, _):
            for k in range(PLANE):
                block_rows = jnp.concatenate([weights[p, k, depth:, :].astype(F32), filler], 0)
                thin[p * PLANE + k] = block_rows.T.astype(BF16)
            return 0

        lax.fori_loop(lowest, highest, one, 0)

    def multiply(j, p, total, factor):
        where = pl.ds(pl.multiple_of(member_at(j) * own_rows, own_rows), own_rows)
        per_core = columns // (PLANE * depth)
        side = p // per_core
        sums = total[where, :]
        for k in range(PLANE):
            span = pl.ds(pl.multiple_of((p % per_core) * (PLANE * depth) + k * depth, depth), depth)
            sums += dot(toks[side, where, span], factor(p, k))
        total[where, :] = sums

    def wide_product(j, p):
        multiply(j, p, wide, lambda p, k: weights[p, k, 0:depth, :])

    def thin_product(j, p):
        multiply(j, p, narrow, lambda p, k: thin[p * PLANE + k])

    def multiply_all(parts, lowest, highest, *products):
        first_part, last_part = parts

        def one(j, p):
            for product in products:
                product(j, p)

        def at(j, _):
            return lax.fori_loop(lowest, highest, lambda p, _: (one(j, p), 0)[1], 0)

        lax.fori_loop(first_part, last_part, at, 0)

    def rest(product):
        multiply_all((0, 3), 0, near_low, product)
        multiply_all((0, 3), near_high, planes, product)

    wide[...] = jnp.zeros_like(wide)
    narrow[...] = jnp.zeros_like(narrow)
    takes = [
        (1, 0, 0, (4, 2)), (2, 1, 2, (5, 1)), (1, 1, 1, None), (2, 0, 3, None),
    ]
    places = [4, 4, 7, 7]
    near_low, near_high = jnp.maximum(plane - (planes - 2), 0), jnp.minimum(plane + planes - 1, planes)
    steps = [(step, j) for step in range(1, planes) for j in range(PLANE)]
    for at, (step, j) in enumerate(steps):
        for take, place in zip(takes, places):
            if min(place, len(steps) - 1) == at:
                token(*take)
        if at == len(steps) - PLANE:
            for copy in own_copies:
                copy.wait()
            for i in range(3):
                from_sibling(i)
            turn(near_low, near_high)
            multiply_all((0, 3), near_low, near_high, wide_product, thin_product)
            token(3, 0, 4)
        if at == len(steps) - 1:
            token(3, 1, 5)
        relay(step, j)
    turn(0, near_low)
    turn(near_high, planes)
    rest(thin_product)
    from_sibling(3)
    multiply_all((3, 4), 0, planes, thin_product)

    me = core * PLANE + member
    for i in range(PLANE):
        part = rows // PLANE
        bc_own[:, i * part : (i + 1) * part] = narrow[i * part : (i + 1) * part, :].T[0:quarter, :].astype(BF16)
    for j in (3, 1, 2):
        send(bc_own, bc_all.at[me], bc_sem.at[me], across[j])
    send(bc_own, bc_all.at[me], bc_sem.at[me], sibling)
    last = bc_own.at[:, pl.ds(rows - GROUP, GROUP)]
    for m in range(PLANE):
        for c in range(2):
            send(last, bc_tail.at[me], bct_sem.at[me], (base + PLANE + m, c), has_above)
    bc_all[me] = bc_own[...]
    rest(wide_product)
    multiply_all((3, 4), 0, planes, wide_product)
    x_last[...] = wide[rows - TAIL : rows, :].astype(BF16)
    send(x_last, x_tail, tail_sem, up, has_above)

    mine = pl.ds(pl.multiple_of(member * channels, channels), channels)
    for copy in loads[2:]:
        copy.wait()
    small[...] = jnp.zeros_like(small)
    for i in range(3):
        small[i : i + 1, 0 : PLANE * heads] = small_in[i]
    own_small = pltpu.roll(small[...], lax.rem(128 - member * heads, 128), 1)
    bias, rate = own_small[0:1, :], own_small[1:2, :]
    skip = spread(own_small, heads, size)[2:3, :]
    taps = taps_x[:, mine]
    own_gain, own_steer = gain[:, mine], steer[:, mine]
    row = lax.broadcasted_iota(jnp.int32, (GROUP, GROUP), 0)
    column = lax.broadcasted_iota(jnp.int32, (GROUP, GROUP), 1)
    causal = row >= column
    lower = causal.astype(BF16)

    def here(at):
        return pl.ds(pl.multiple_of(at * GROUP, GROUP), GROUP)

    def steps_of(at, _):
        raw = pltpu.roll(narrow[here(at), :], 128 - quarter - member * heads, 1) + bias
        dt = jnp.maximum(raw, 0.0) + jnp.log1p(jnp.exp(-jnp.abs(raw)))
        a = -dt * rate
        one = a.astype(BF16)
        rest = a - one.astype(F32)
        two = rest.astype(BF16)
        three = (rest - two.astype(F32)).astype(BF16)
        s_keep[here(at), :] = dot(lower, one) + (dot(lower, two) + dot(lower, three))
        dt_keep[here(at), :] = dt
        x_pad[pl.ds(pl.multiple_of(at * GROUP + TAIL, TAIL), GROUP), :] = wide[here(at), :].astype(BF16).astype(F32)
        return 0

    lax.fori_loop(0, blocks, steps_of, 0, unroll=4)
    for j in (1, 2, 3):
        slot = core * PLANE + members[j]
        arrived(bc_all.at[slot], bc_sem.at[slot])
        send(bc_all.at[slot], bc_all.at[slot], bc_sem.at[slot], sibling)

    @pl.when(jnp.logical_not(has_below))
    def _():
        x_tail[...] = jnp.zeros_like(x_tail)
        bc_tail[...] = jnp.zeros_like(bc_tail)

    arrived(x_tail, tail_sem, has_below)
    x_pad[0:TAIL, :] = x_tail[...].astype(F32)

    def convolved(at, _):
        x_conv[here(at), :] = smooth(x_pad, at, taps)
        return 0

    lax.fori_loop(0, blocks, convolved, 0, unroll=4)

    for j in range(PLANE):
        slot = (1 - core) * PLANE + members[j]
        arrived(bc_all.at[slot], bc_sem.at[slot])
    for sender in range(2 * PLANE):
        arrived(bc_tail.at[sender], bct_sem.at[sender], has_below)
    bc_pad[0:TAIL, :] = bc_tail[...].astype(F32).reshape(2 * N, GROUP).T[GROUP - TAIL :, :]

    def unturned(at, _):
        turned = bc_all[:, :, here(at)].astype(F32).reshape(2 * N, GROUP)
        bc_pad[pl.ds(pl.multiple_of(at * GROUP + TAIL, TAIL), GROUP), :] = turned.T
        return 0

    lax.fori_loop(0, blocks, unturned, 0, unroll=4)

    def advance(at, carry):
        state, log = carry
        bc = smooth(bc_pad, at, taps_bc[...])
        bc_conv[here(at), :] = bc
        s = s_keep[here(at), :]
        states[at] = state
        logs[at] = log
        end = s[GROUP - 1 : GROUP, :]
        weight = spread(jnp.exp(end - s) * dt_keep[here(at), :], heads, size)
        scaled = (x_conv[here(at), :].astype(F32) * weight).astype(BF16)
        b_turned = bc[:, :N].astype(F32).T.astype(BF16)
        ended = jnp.broadcast_to(end, (8, 128))
        state = spread(jnp.exp(ended), heads, size)[0:1, :] * state + dot(b_turned, scaled)
        return state, log + ended

    zeros = (jnp.zeros((N, channels), F32), jnp.zeros((8, 128), F32))
    state, log = lax.fori_loop(0, blocks, advance, zeros, unroll=4)
    state_out[...] = state.astype(BF16)
    total_out[...] = log
    for j in range(1, planes):
        other = (far[j] * PLANE + member, core)
        send(state_out, state_in.at[planes - j], state_sem.at[planes - j], other)
        send(total_out, total_in.at[planes - j], total_sem.at[planes - j], other)

    def inside(at, _):
        x = x_conv[here(at), :]
        bc = bc_conv[here(at), :]
        s = s_keep[here(at), :]
        s_turned = s.T
        dt_turned = dt_keep[here(at), :].T
        scores = lax.dot_general(bc[:, N:], bc[:, :N], (((1,), (1,)), ((), ())), preferred_element_type=F32)
        parts = []
        for h in range(heads):
            differ = s[:, h : h + 1] - s_turned[h : h + 1, :]
            decays = jnp.where(causal, jnp.exp(jnp.where(causal, differ, 0.0)), 0.0)
            mixing = (scores * decays * dt_turned[h : h + 1, :]).astype(BF16)
            parts.append(dot(mixing, x[:, h * size : (h + 1) * size]))
        y_keep[here(at), :] = jnp.concatenate(parts, 1) + skip * x.astype(F32)
        return 0

    lax.fori_loop(0, blocks, inside, 0, unroll=4)

    entering = first[...].T
    for j in range(1, planes):
        arrived(state_in.at[j], state_sem.at[j])
        arrived(total_in.at[j], total_sem.at[j])
    for j in range(1, planes):
        later = spread(jnp.exp(total_in[j]), heads, size)[0:1, :] * entering + state_in[j].astype(F32)
        entering = jnp.where(far[j] < plane, later, entering)

    group_of = lax.broadcasted_iota(jnp.int32, (2, channels, channels), 1) // size
    same = (group_of[0] == lax.broadcasted_iota(jnp.int32, (channels, channels), 1) // size).astype(BF16)

    def finish(at):
        s = s_keep[here(at), :]
        c = bc_conv[here(at), :][:, N:]
        state = states[at] + spread(jnp.exp(logs[at]), heads, size)[0:1, :] * entering
        y = y_keep[here(at), :] + spread(jnp.exp(s), heads, size) * split_dot(c, state)
        square = y * y
        high = square.astype(BF16)
        low = (square - high.astype(F32)).astype(BF16)
        mean = (dot(high, same) + dot(low, same)) * (1.0 / size)
        scaled = y * lax.rsqrt(mean + EPSILON) * own_gain
        normed[here(at), :] = scaled.astype(BF16)
        along = jnp.sum(scaled * own_steer, axis=1, keepdims=True)
        partial[at] = jnp.broadcast_to(along, (GROUP, GROUP)).T[0:8, :]

    for j in (3, 1, 2, 0):
        target = members[j]
        lax.fori_loop(0, per_member, lambda i, _: (finish(target * per_member + i), 0)[1], 0, unroll=2)
        pieces = partial.at[pl.ds(target * per_member, per_member)]
        if j:
            chunk = normed.at[pl.ds(pl.multiple_of(target * own_rows, own_rows), own_rows)]
            send(chunk, normed_in.at[member], normed_sem.at[j], (base + target, core))
            send(pieces, partial_in.at[0, j], partial_sem.at[0, j], (base + target, core))
        send(pieces, partial_in.at[1, j], partial_sem.at[1, j], (base + target, 1 - core))
    normed_in[member] = normed[pl.ds(pl.multiple_of(member * own_rows, own_rows), own_rows), :]
    penalty = partial[pl.ds(member * per_member, per_member)]
    for j in range(PLANE):
        if j:
            arrived(normed_in.at[members[j]], normed_sem.at[j])
            arrived(partial_in.at[0, j], partial_sem.at[0, j])
            penalty = penalty + partial_in[0, j]
        arrived(partial_in.at[1, j], partial_sem.at[1, j])
        penalty = penalty + partial_in[1, j]
    penalty = penalty * (1.0 / (channels * PLANE * lax.axis_size("tp")) ** 0.5)
    for i in range(per_member):
        turned = jnp.broadcast_to(penalty[i][0:1, :], (GROUP, GROUP)).T
        turned = jnp.concatenate([turned] * (channels // GROUP), 1)
        span = pl.ds(i * GROUP, GROUP)
        for j in range(PLANE):
            value = normed_in[j, span, :].astype(F32) - turned * steer[:, j * channels : (j + 1) * channels]
            out_ref[span, j * channels : (j + 1) * channels] = value.astype(BF16)
    for copy, when in started:
        if when is None:
            copy.wait_send()
        else:
            pl.when(when)(lambda copy=copy: copy.wait_send())


def per_device(tokens, x_weight, bc_weight, dt_weight, conv_x, conv_bc, dt_bias, decay_rate, d_skip, norm_gain, initial_state, steer):
    planes = lax.axis_size("seq") // PLANE
    own_rows, columns = tokens.shape
    depth, all_channels = x_weight.shape
    all_heads = dt_weight.shape[1]
    channels, heads = all_channels // PLANE, all_heads // PLANE
    rows = own_rows * PLANE
    blocks = rows // GROUP
    quarter = bc_weight.shape[1] // PLANE

    vmem = pl.BlockSpec(memory_space=pltpu.VMEM)
    far = pl.BlockSpec(memory_space=pltpu.HBM)
    dma = pltpu.SemaphoreType.DMA
    out = pl.pallas_call(
        functools.partial(layer_kernel, planes, heads),
        out_shape=jax.ShapeDtypeStruct((own_rows, all_channels), BF16),
        in_specs=[far] * 12,
        out_specs=vmem,
        scratch_shapes=[
            pltpu.VMEM(bc_weight.shape, BF16),
            pltpu.VMEM((all_heads, depth), BF16),
            pltpu.VMEM((PLANE, quarter + TAIL, depth), BF16),
            pltpu.VMEM(conv_x.shape, F32),
            pltpu.VMEM(conv_bc.shape, F32),
            pltpu.VMEM((3, 1, all_heads), F32),
            pltpu.VMEM((8, 128), F32),
            pltpu.VMEM((1, all_channels), F32),
            pltpu.VMEM((channels, N), F32),
            pltpu.VMEM((1, all_channels), F32),
            dma((10,)),
            pltpu.VMEM((2, rows, columns), BF16),
            pltpu.VMEM((planes, PLANE, depth + quarter + TAIL, channels), BF16),
            pltpu.VMEM((planes * PLANE, depth, 128), BF16),
            pltpu.VMEM((rows, channels), F32),
            pltpu.VMEM((rows, 128), F32),
            pltpu.VMEM((TAIL, channels), BF16),
            pltpu.VMEM((TAIL, channels), BF16),
            pltpu.VMEM((quarter, rows), BF16),
            pltpu.VMEM((2 * PLANE, quarter, rows), BF16),
            pltpu.VMEM((2 * PLANE, quarter, GROUP), BF16),
            pltpu.VMEM((rows + TAIL, channels), F32),
            pltpu.VMEM((rows + TAIL, 2 * N), F32),
            pltpu.VMEM((rows, channels), BF16),
            pltpu.VMEM((rows, 2 * N), BF16),
            pltpu.VMEM((rows, 128), F32),
            pltpu.VMEM((rows, 128), F32),
            pltpu.VMEM((blocks, N, channels), F32),
            pltpu.VMEM((blocks, 8, 128), F32),
            pltpu.VMEM((rows, channels), F32),
            pltpu.VMEM((N, channels), BF16),
            pltpu.VMEM((8, 128), F32),
            pltpu.VMEM((planes, N, channels), BF16),
            pltpu.VMEM((planes, 8, 128), F32),
            pltpu.VMEM((rows, channels), BF16),
            pltpu.VMEM((blocks, 8, GROUP), F32),
            pltpu.VMEM((PLANE, own_rows, channels), BF16),
            pltpu.VMEM((2, PLANE, blocks // PLANE, 8, GROUP), F32),
            dma((64 + 10 * planes,)),
            dma((6,)),
            dma((PLANE, 2)),
            dma((PLANE,)),
            dma((2, planes, PLANE)),
            dma((3,)),
            dma(()),
            dma((2 * PLANE,)),
            dma((2 * PLANE,)),
            dma((planes,)),
            dma((planes,)),
            dma((PLANE,)),
            dma((2, PLANE)),
        ],
        compiler_params=pltpu.CompilerParams(collective_id=0, has_side_effects=True, vmem_limit_bytes=60 * 2**20),
    )(
        tokens, x_weight, bc_weight, dt_weight.T, conv_x, conv_bc, dt_bias[None, :], decay_rate[None, :], d_skip[None, :],
        norm_gain[None, :], initial_state.reshape(all_channels, N), steer[None, :],
    )
    return out


def solution(mesh):
    placed = (
        P("seq", "tp"),
        P("seq", "tp"),
        P("seq", "tp"),
        P("seq", "tp"),
        P(None, "tp"),
        P(),
        P("tp"),
        P("tp"),
        P("tp"),
        P("tp"),
        P("tp", None, None),
        P("tp"),
    )
    planar = mesh.shape["tp"] == 2 and mesh.shape["seq"] % PLANE == 0
    return jax.shard_map(
        per_device if planar else portable, mesh=mesh, in_specs=placed, out_specs=P("seq", "tp"), check_vma=False
    )
```

```python
import functools

import jax
import jax.numpy as jnp
from jax import lax
from jax.experimental import pallas as pl
from jax.experimental.pallas import tpu as pltpu
from jax.sharding import PartitionSpec as P

MESH = pl.DeviceIdType.MESH
PLANE = 4
TAIL = 16
F32 = jnp.float32
BF16 = jnp.bfloat16

N = 128
GROUP = 128


EPSILON = 1e-05


def passed_along(value, axis, steps):
    count = lax.axis_size(axis)
    first, last = (max(0, -steps), min(count, count - steps))
    return lax.ppermute(value, axis, [(source, source + steps) for source in range(first, last)])


def prefix(x, axis, combine, identity):
    count, mine = (lax.axis_size(axis), lax.axis_index(axis))
    everything = jax.tree.map(
        lambda part, kind: lax.all_gather(part.astype(kind), axis), x, (jnp.bfloat16, jnp.bfloat16)
    )
    start = jax.tree.map(
        lambda part, zero: jnp.broadcast_to(jnp.asarray(zero, part.dtype), part.shape), x, identity
    )

    def turn(k, before):
        reached = k < mine
        new = combine(
            before, jax.tree.map(lambda part, own: part[k].astype(own.dtype), everything, x)
        )
        return jax.tree.map(lambda a, b: jnp.where(reached, a, b), new, before)

    return lax.fori_loop(0, count, turn, start)


def convolve(extended, kernel):
    kernel_rows = kernel.shape[0]
    length = extended.shape[0] - kernel_rows + 1
    summed = kernel[0] * extended[0:length].astype(jnp.float32)
    for offset in range(1, kernel_rows):
        summed = summed + kernel[offset] * extended[offset : offset + length].astype(jnp.float32)
    return jax.nn.silu(summed).astype(jnp.bfloat16)


def block_update(carry_state, inputs):
    x_block, b_block, c_block, a_block, dt_block = inputs
    length = a_block.shape[0]
    cumulative = jnp.cumsum(a_block, axis=0)
    scores = jnp.dot(c_block, b_block.T, preferred_element_type=jnp.float32)
    causal = lax.broadcasted_iota(jnp.int32, (length, length), 0) >= lax.broadcasted_iota(
        jnp.int32, (length, length), 1
    )
    differ = cumulative[:, None, :] - cumulative[None, :, :]
    decays = jnp.where(causal[:, :, None], jnp.exp(jnp.where(causal[:, :, None], differ, 0.0)), 0.0)
    mixing = (scores[:, :, None] * decays * dt_block[None, :, :]).astype(jnp.bfloat16)
    inside = jnp.einsum("tsh,shp->thp", mixing, x_block, preferred_element_type=jnp.float32)
    carried_in = jnp.einsum(
        "tn,hpn->thp", c_block.astype(jnp.float32), carry_state, precision=lax.Precision.HIGHEST
    )
    outputs = inside + jnp.exp(cumulative)[:, :, None] * carried_in
    to_end = jnp.exp(cumulative[-1][None, :] - cumulative) * dt_block
    scaled = (x_block.astype(jnp.float32) * to_end[:, :, None]).astype(jnp.bfloat16)
    added_state = jnp.einsum("shp,sn->hpn", scaled, b_block, preferred_element_type=jnp.float32)
    return (jnp.exp(cumulative[-1])[:, None, None] * carry_state + added_state, outputs)


def combine_carry(earlier, later):
    return (earlier[0] * later[0], later[0][:, None, None] * earlier[1] + later[1])


def portable(
    tokens,
    x_weight,
    bc_weight,
    dt_weight,
    conv_x,
    conv_bc,
    dt_bias,
    decay_rate,
    d_skip,
    norm_gain,
    initial_state,
    steer,
):
    features = lax.all_gather(tokens, "tp", axis=1, tiled=True)
    rim_rows = conv_x.shape[0] - 1
    local_tokens = features.shape[0]
    head_count = dt_weight.shape[1]
    channels = x_weight.shape[1]
    head_size = channels // head_count
    bc_panel = lax.all_gather(bc_weight, "tp", axis=1, tiled=True)
    previous = passed_along(features[local_tokens - rim_rows :], "seq", 1)
    source = jnp.concatenate([previous, features], 0)
    x_sums = jnp.dot(
        source,
        lax.all_gather(x_weight, "seq", axis=0, tiled=True),
        preferred_element_type=jnp.float32,
    )
    bc_sums = jnp.dot(
        source,
        lax.all_gather(bc_panel, "seq", axis=0, tiled=True),
        preferred_element_type=jnp.float32,
    )
    dt_sums = jnp.dot(
        source,
        lax.all_gather(dt_weight, "seq", axis=0, tiled=True),
        preferred_element_type=jnp.float32,
    )
    x_pre = x_sums.astype(jnp.bfloat16)
    bc_pre = bc_sums.astype(jnp.bfloat16)
    dt_raw = dt_sums[rim_rows:]
    x_conv = convolve(x_pre, conv_x)
    bc_conv = convolve(bc_pre, conv_bc)
    b_values = bc_conv[:, :N]
    c_values = bc_conv[:, N:]
    step_size = jax.nn.softplus(dt_raw + dt_bias[None, :])
    log_decay = -step_size * decay_rate[None, :]
    blocks = local_tokens // GROUP
    x_heads = x_conv.reshape(local_tokens, head_count, head_size)
    inputs = (
        x_heads.reshape(blocks, GROUP, head_count, head_size),
        b_values.reshape(blocks, GROUP, N),
        c_values.reshape(blocks, GROUP, N),
        log_decay.reshape(blocks, GROUP, head_count),
        step_size.reshape(blocks, GROUP, head_count),
    )
    zero_state = jnp.zeros((head_count, head_size, N), jnp.float32)
    local_state, local_out = lax.scan(block_update, zero_state, inputs)
    running = jnp.cumsum(log_decay, axis=0)
    local_decay = jnp.exp(running[-1])
    identity = (
        jnp.ones((head_count,), jnp.float32),
        jnp.zeros((head_count, head_size, N), jnp.float32),
    )
    prefix_decay, prefix_state = prefix((local_decay, local_state), "seq", combine_carry, identity)
    entering = prefix_decay[:, None, None] * initial_state + prefix_state
    from_entering = jnp.einsum(
        "tn,hpn->thp", c_values.astype(jnp.float32), entering, precision=lax.Precision.HIGHEST
    )
    outputs = (
        local_out.reshape(local_tokens, head_count, head_size)
        + jnp.exp(running)[:, :, None] * from_entering
        + d_skip[None, :, None] * x_heads.astype(jnp.float32)
    )
    mean_square = jnp.mean(outputs * outputs, axis=-1, keepdims=True)
    normed = (outputs * lax.rsqrt(mean_square + EPSILON)).reshape(
        local_tokens, channels
    ) * norm_gain[None, :]
    partial_dot = jnp.sum(normed * steer[None, :], axis=1)
    total_dot = lax.psum(partial_dot, "tp")
    penalty = total_dot / jnp.sqrt(jnp.float32(channels * lax.axis_size("tp")))
    return (normed - penalty[:, None] * steer[None, :]).astype(jnp.bfloat16)


def dot(a, b):
    return jnp.dot(a, b, preferred_element_type=F32)


def split_dot(a, b):
    high = b.astype(BF16)
    low = (b - high.astype(F32)).astype(BF16)
    return dot(a, high) + dot(a, low)


def smooth(ref, at, taps):
    rows = ref[pl.ds(pl.multiple_of(at * GROUP + TAIL - 8, 8), GROUP + 8), :]
    width = taps.shape[0]
    summed = taps[0:1, :] * rows[9 - width : 9 - width + GROUP]
    for k in range(1, width):
        summed = summed + taps[k : k + 1, :] * rows[9 - width + k : 9 - width + k + GROUP]
    return (summed / (1.0 + jnp.exp(-summed))).astype(BF16)


def spread(values, heads, size):
    head = lax.broadcasted_iota(jnp.int32, (128, heads * size), 0)
    lane = lax.broadcasted_iota(jnp.int32, (128, heads * size), 1)
    chosen = (head == lane // size).astype(BF16)
    high = values.astype(BF16)
    low = (values - high.astype(F32)).astype(BF16)
    return dot(high, chosen) + dot(low, chosen)


def layer_kernel(
    planes, heads, tok_ref, xw_ref, bcw_hbm, dtw_hbm, taps_x_hbm, taps_bc_hbm, bias_hbm, rate_hbm, skip_hbm, gain_hbm, first_hbm, steer_hbm, out_ref,
    bcw, dtw, pack_ref, taps_x, taps_bc, small_in, small, gain, first, steer, load_sem,
    toks, weights, thin, wide, narrow, x_tail, x_last, bc_own, bc_all, bc_tail,
    x_pad, bc_pad, x_conv, bc_conv, s_keep, dt_keep, states, logs, y_keep, state_out, total_out, state_in, total_in,
    normed, partial, normed_in, partial_in,
    send_sem, tok_sem, sib_sem, swap_sem, line_sem, own_sem, tail_sem, bct_sem, bc_sem, state_sem, total_sem, normed_sem, partial_sem,
):
    seq, core = lax.axis_index("seq"), lax.axis_index("tp")
    plane, member = lax.div(seq, PLANE), lax.rem(seq, PLANE)
    base = plane * PLANE
    own_rows, columns = tok_ref.shape
    rows = own_rows * PLANE
    half = own_rows // 2
    depth = xw_ref.shape[0]
    channels = weights.shape[3]
    size = channels // heads
    quarter = weights.shape[2] - depth - TAIL
    blocks = rows // GROUP
    per_member = blocks // PLANE
    my_x, my_y = lax.rem(member, 2), lax.div(member, 2)

    def member_at(j):
        return lax.rem(my_y + j // 2, 2) * 2 + lax.rem(my_x + j % 2, 2)

    members = [member_at(j) for j in range(PLANE)]
    far = [lax.rem(plane + j, planes) for j in range(planes)]
    has_below, has_above = plane > 0, plane < planes - 1

    loads = [
        (bcw_hbm, bcw), (dtw_hbm, dtw), (taps_x_hbm, taps_x), (taps_bc_hbm, taps_bc), (bias_hbm, small_in.at[0]),
        (rate_hbm, small_in.at[1]), (skip_hbm, small_in.at[2]), (gain_hbm, gain), (steer_hbm, steer),
        (first_hbm.at[pl.ds(pl.multiple_of(member * channels, channels), channels)], first),
    ]
    loads = [pltpu.make_async_copy(source, target, load_sem.at[i]) for i, (source, target) in enumerate(loads)]
    for copy in loads:
        copy.start()
    barrier = pltpu.get_barrier_semaphore()

    def greet(s, c):
        pl.semaphore_signal(barrier, inc=1, device_id=(s, c), device_id_type=MESH)

    for j in range(PLANE):
        greet(base + members[j], 1 - core)
        if j:
            greet(base + members[j], core)

    @pl.when(has_below)
    def _():
        for m in range(PLANE):
            for c in range(2):
                greet(base - PLANE + m, c)

    @pl.when(has_above)
    def _():
        for m in range(PLANE):
            for c in range(2):
                greet(base + PLANE + m, c)

    greeted = 2 * PLANE - 1 + jnp.where(has_below, 2 * PLANE, 0) + jnp.where(has_above, 2 * PLANE, 0)
    for j in range(1, planes):
        distant = jnp.abs(far[j] - plane) > 1
        pl.when(distant)(lambda j=j: greet(far[j] * PLANE + member, core))
        greeted = greeted + jnp.where(distant, 1, 0)
    loads[0].wait()
    loads[1].wait()
    turned = bcw[...].astype(F32).T.astype(BF16)
    for m in range(PLANE):
        pack_ref[m, 0:quarter, :] = turned[m * quarter : (m + 1) * quarter]
        pack_ref[m, quarter:, :] = dtw[...]
    pl.semaphore_wait(barrier, greeted)

    started = []

    def send(source, target, sem, device, when=None):
        copy = pltpu.make_async_remote_copy(
            src_ref=source, dst_ref=target, send_sem=send_sem.at[len(started)], recv_sem=sem,
            device_id=device, device_id_type=MESH,
        )
        started.append((copy, when))
        if when is None:
            copy.start()
        else:
            pl.when(when)(lambda: copy.start())

    def arrived(target, sem, when=None):
        copy = pltpu.make_async_remote_copy(
            src_ref=target, dst_ref=target, send_sem=send_sem.at[0], recv_sem=sem,
            device_id=(seq, 1 - core), device_id_type=MESH,
        )
        if when is None:
            copy.wait_recv()
        else:
            pl.when(when)(lambda: copy.wait_recv())

    def piece(c, j, h):
        return toks.at[c, pl.ds(pl.multiple_of(members[j] * own_rows + h * half, half), half)]

    def own_piece(h):
        return tok_ref.at[pl.ds(h * half, half)]

    def block(p, j):
        return weights.at[p, members[j]]

    across = [(base + members[j], core) for j in range(PLANE)]
    up, down, sibling = (seq + PLANE, core), (seq - PLANE, core), (seq, 1 - core)

    def quarter_of(m):
        return xw_ref.at[:, pl.ds(pl.multiple_of(m * channels, channels), channels)]

    def wide_part(m, *where):
        send(quarter_of(m), weights.at[plane, member, pl.ds(0, depth)], *where)

    def thin_part(m, *where):
        send(pack_ref.at[m], weights.at[plane, member, pl.ds(depth, quarter + TAIL)], *where)

    own_copies = [
        pltpu.make_async_copy(quarter_of(member), weights.at[plane, member, pl.ds(0, depth)], own_sem.at[0]),
        pltpu.make_async_copy(pack_ref.at[member], weights.at[plane, member, pl.ds(depth, quarter + TAIL)], own_sem.at[1]),
        pltpu.make_async_copy(tok_ref, toks.at[core, pl.ds(pl.multiple_of(member * own_rows, own_rows), own_rows)], own_sem.at[2]),
    ]
    own_copies[0].start()
    own_copies[2].start()

    def first_parts(part):
        for j in (1, 2, 3):
            part(members[j], swap_sem.at[j], across[j])
        part(member, line_sem.at[0, 1, 0], up, has_above)
        part(member, line_sem.at[1, 1, 0], down, has_below)

    first_parts(wide_part)
    own_copies[1].start()
    first_parts(thin_part)
    send(own_piece(0), piece(core, 0, 0), tok_sem.at[0], across[1])
    send(own_piece(1), piece(core, 0, 1), tok_sem.at[2], across[2])
    send(own_piece(1), piece(core, 0, 1), tok_sem.at[1], across[1])
    send(own_piece(0), piece(core, 0, 0), tok_sem.at[3], across[2])
    send(own_piece(0), piece(core, 0, 0), sib_sem.at[0, 0], sibling)
    send(own_piece(1), piece(core, 0, 1), sib_sem.at[0, 1], sibling)
    for j in (1, 2, 3):
        arrived(block(plane, j), swap_sem.at[j])
        send(block(plane, j), block(plane, j), line_sem.at[0, 1, j], up, has_above)
        send(block(plane, j), block(plane, j), line_sem.at[1, 1, j], down, has_below)

    def relay(step, j):
        lower, upper = plane - step, plane + step
        arrived(block(jnp.maximum(lower, 0), j), line_sem.at[0, step, j], lower >= 0)
        arrived(block(jnp.minimum(upper, planes - 1), j), line_sem.at[1, step, j], upper < planes)
        if step < planes - 1:
            low = block(jnp.maximum(lower, 0), j)
            high = block(jnp.minimum(upper, planes - 1), j)
            send(low, low, line_sem.at[0, step + 1, j], up, jnp.logical_and(lower >= 0, has_above))
            send(high, high, line_sem.at[1, step + 1, j], down, jnp.logical_and(upper < planes, has_below))

    def token(j, h, index, forward=None):
        here = piece(core, j, h)
        arrived(here, tok_sem.at[index])
        if forward is not None:
            send(here, here, tok_sem.at[forward[0]], across[forward[1]])
        send(here, here, sib_sem.at[j, h], sibling)

    def from_sibling(j):
        for h in range(2):
            arrived(piece(1 - core, j, h), sib_sem.at[j, h])

    filler = jnp.zeros((128 - quarter - TAIL, depth), F32)

    def turn(lowest, highest):
        def one(p, _):
            for k in range(PLANE):
                block_rows = jnp.concatenate([weights[p, k, depth:, :].astype(F32), filler], 0)
                thin[p * PLANE + k] = block_rows.T.astype(BF16)
            return 0

        lax.fori_loop(lowest, highest, one, 0)

    def multiply(j, p, total, factor):
        where = pl.ds(pl.multiple_of(member_at(j) * own_rows, own_rows), own_rows)
        per_core = columns // (PLANE * depth)
        side = p // per_core
        sums = total[where, :]
        for k in range(PLANE):
            span = pl.ds(pl.multiple_of((p % per_core) * (PLANE * depth) + k * depth, depth), depth)
            sums += dot(toks[side, where, span], factor(p, k))
        total[where, :] = sums

    def wide_product(j, p):
        multiply(j, p, wide, lambda p, k: weights[p, k, 0:depth, :])

    def thin_product(j, p):
        multiply(j, p, narrow, lambda p, k: thin[p * PLANE + k])

    def multiply_all(parts, lowest, highest, *products):
        first_part, last_part = parts

        def one(j, p):
            for product in products:
                product(j, p)

        def at(j, _):
            return lax.fori_loop(lowest, highest, lambda p, _: (one(j, p), 0)[1], 0)

        lax.fori_loop(first_part, last_part, at, 0)

    def rest(product):
        multiply_all((0, 3), 0, near_low, product)
        multiply_all((0, 3), near_high, planes, product)

    wide[...] = jnp.zeros_like(wide)
    narrow[...] = jnp.zeros_like(narrow)
    takes = [
        (1, 0, 0, (4, 2)), (2, 1, 2, (5, 1)), (1, 1, 1, None), (2, 0, 3, None),
    ]
    places = [4, 4, 7, 7]
    near_low, near_high = jnp.maximum(plane - (planes - 2), 0), jnp.minimum(plane + planes - 1, planes)
    steps = [(step, j) for step in range(1, planes) for j in range(PLANE)]
    for at, (step, j) in enumerate(steps):
        for take, place in zip(takes, places):
            if min(place, len(steps) - 1) == at:
                token(*take)
        if at == len(steps) - PLANE:
            for copy in own_copies:
                copy.wait()
            for i in range(3):
                from_sibling(i)
            turn(near_low, near_high)
            multiply_all((0, 3), near_low, near_high, wide_product, thin_product)
            token(3, 0, 4)
        if at == len(steps) - 1:
            token(3, 1, 5)
        relay(step, j)
    turn(0, near_low)
    turn(near_high, planes)
    rest(thin_product)
    from_sibling(3)
    multiply_all((3, 4), 0, planes, thin_product)

    me = core * PLANE + member
    for i in range(PLANE):
        part = rows // PLANE
        bc_own[:, i * part : (i + 1) * part] = narrow[i * part : (i + 1) * part, :].T[0:quarter, :].astype(BF16)
    for j in (3, 1, 2):
        send(bc_own, bc_all.at[me], bc_sem.at[me], across[j])
    send(bc_own, bc_all.at[me], bc_sem.at[me], sibling)
    last = bc_own.at[:, pl.ds(rows - GROUP, GROUP)]
    for m in range(PLANE):
        for c in range(2):
            send(last, bc_tail.at[me], bct_sem.at[me], (base + PLANE + m, c), has_above)
    bc_all[me] = bc_own[...]
    rest(wide_product)
    multiply_all((3, 4), 0, planes, wide_product)
    x_last[...] = wide[rows - TAIL : rows, :].astype(BF16)
    send(x_last, x_tail, tail_sem, up, has_above)

    mine = pl.ds(pl.multiple_of(member * channels, channels), channels)
    for copy in loads[2:]:
        copy.wait()
    small[...] = jnp.zeros_like(small)
    for i in range(3):
        small[i : i + 1, 0 : PLANE * heads] = small_in[i]
    own_small = pltpu.roll(small[...], lax.rem(128 - member * heads, 128), 1)
    bias, rate = own_small[0:1, :], own_small[1:2, :]
    skip = spread(own_small, heads, size)[2:3, :]
    taps = taps_x[:, mine]
    own_gain, own_steer = gain[:, mine], steer[:, mine]
    row = lax.broadcasted_iota(jnp.int32, (GROUP, GROUP), 0)
    column = lax.broadcasted_iota(jnp.int32, (GROUP, GROUP), 1)
    causal = row >= column
    lower = causal.astype(BF16)

    def here(at):
        return pl.ds(pl.multiple_of(at * GROUP, GROUP), GROUP)

    def steps_of(at, _):
        raw = pltpu.roll(narrow[here(at), :], 128 - quarter - member * heads, 1) + bias
        dt = jnp.maximum(raw, 0.0) + jnp.log1p(jnp.exp(-jnp.abs(raw)))
        a = -dt * rate
        one = a.astype(BF16)
        rest = a - one.astype(F32)
        two = rest.astype(BF16)
        three = (rest - two.astype(F32)).astype(BF16)
        s_keep[here(at), :] = dot(lower, one) + (dot(lower, two) + dot(lower, three))
        dt_keep[here(at), :] = dt
        x_pad[pl.ds(pl.multiple_of(at * GROUP + TAIL, TAIL), GROUP), :] = wide[here(at), :].astype(BF16).astype(F32)
        return 0

    lax.fori_loop(0, blocks, steps_of, 0, unroll=8)
    for j in (1, 2, 3):
        slot = core * PLANE + members[j]
        arrived(bc_all.at[slot], bc_sem.at[slot])
        send(bc_all.at[slot], bc_all.at[slot], bc_sem.at[slot], sibling)

    @pl.when(jnp.logical_not(has_below))
    def _():
        x_tail[...] = jnp.zeros_like(x_tail)
        bc_tail[...] = jnp.zeros_like(bc_tail)

    arrived(x_tail, tail_sem, has_below)
    x_pad[0:TAIL, :] = x_tail[...].astype(F32)

    def convolved(at, _):
        x_conv[here(at), :] = smooth(x_pad, at, taps)
        return 0

    lax.fori_loop(0, blocks, convolved, 0, unroll=8)

    for j in range(PLANE):
        slot = (1 - core) * PLANE + members[j]
        arrived(bc_all.at[slot], bc_sem.at[slot])
    for sender in range(2 * PLANE):
        arrived(bc_tail.at[sender], bct_sem.at[sender], has_below)
    bc_pad[0:TAIL, :] = bc_tail[...].astype(F32).reshape(2 * N, GROUP).T[GROUP - TAIL :, :]

    def unturned(at, _):
        turned = bc_all[:, :, here(at)].astype(F32).reshape(2 * N, GROUP)
        bc_pad[pl.ds(pl.multiple_of(at * GROUP + TAIL, TAIL), GROUP), :] = turned.T
        return 0

    lax.fori_loop(0, blocks, unturned, 0, unroll=8)

    def advance(at, carry):
        state, log = carry
        bc = smooth(bc_pad, at, taps_bc[...])
        bc_conv[here(at), :] = bc
        s = s_keep[here(at), :]
        states[at] = state
        logs[at] = log
        end = s[GROUP - 1 : GROUP, :]
        weight = spread(jnp.exp(end - s) * dt_keep[here(at), :], heads, size)
        scaled = (x_conv[here(at), :].astype(F32) * weight).astype(BF16)
        b_turned = bc[:, :N].astype(F32).T.astype(BF16)
        ended = jnp.broadcast_to(end, (8, 128))
        state = spread(jnp.exp(ended), heads, size)[0:1, :] * state + dot(b_turned, scaled)
        return state, log + ended

    zeros = (jnp.zeros((N, channels), F32), jnp.zeros((8, 128), F32))
    state, log = lax.fori_loop(0, blocks, advance, zeros, unroll=8)
    state_out[...] = state.astype(BF16)
    total_out[...] = log
    for j in range(1, planes):
        other = (far[j] * PLANE + member, core)
        send(state_out, state_in.at[planes - j], state_sem.at[planes - j], other)
        send(total_out, total_in.at[planes - j], total_sem.at[planes - j], other)

    def inside(at, _):
        x = x_conv[here(at), :]
        bc = bc_conv[here(at), :]
        s = s_keep[here(at), :]
        s_turned = s.T
        dt_turned = dt_keep[here(at), :].T
        scores = lax.dot_general(bc[:, N:], bc[:, :N], (((1,), (1,)), ((), ())), preferred_element_type=F32)
        parts = []
        for h in range(heads):
            differ = s[:, h : h + 1] - s_turned[h : h + 1, :]
            decays = jnp.where(causal, jnp.exp(jnp.where(causal, differ, 0.0)), 0.0)
            mixing = (scores * decays * dt_turned[h : h + 1, :]).astype(BF16)
            parts.append(dot(mixing, x[:, h * size : (h + 1) * size]))
        y_keep[here(at), :] = jnp.concatenate(parts, 1) + skip * x.astype(F32)
        return 0

    lax.fori_loop(0, blocks, inside, 0, unroll=8)

    entering = first[...].T
    for j in range(1, planes):
        arrived(state_in.at[j], state_sem.at[j])
        arrived(total_in.at[j], total_sem.at[j])
    for j in range(1, planes):
        later = spread(jnp.exp(total_in[j]), heads, size)[0:1, :] * entering + state_in[j].astype(F32)
        entering = jnp.where(far[j] < plane, later, entering)

    group_of = lax.broadcasted_iota(jnp.int32, (2, channels, channels), 1) // size
    same = (group_of[0] == lax.broadcasted_iota(jnp.int32, (channels, channels), 1) // size).astype(BF16)

    def finish(at):
        s = s_keep[here(at), :]
        c = bc_conv[here(at), :][:, N:]
        state = states[at] + spread(jnp.exp(logs[at]), heads, size)[0:1, :] * entering
        y = y_keep[here(at), :] + spread(jnp.exp(s), heads, size) * split_dot(c, state)
        square = y * y
        high = square.astype(BF16)
        low = (square - high.astype(F32)).astype(BF16)
        mean = (dot(high, same) + dot(low, same)) * (1.0 / size)
        scaled = y * lax.rsqrt(mean + EPSILON) * own_gain
        normed[here(at), :] = scaled.astype(BF16)
        along = jnp.sum(scaled * own_steer, axis=1, keepdims=True)
        partial[at] = jnp.broadcast_to(along, (GROUP, GROUP)).T[0:8, :]

    for j in (3, 1, 2, 0):
        target = members[j]
        lax.fori_loop(0, per_member, lambda i, _: (finish(target * per_member + i), 0)[1], 0, unroll=2)
        pieces = partial.at[pl.ds(target * per_member, per_member)]
        if j:
            chunk = normed.at[pl.ds(pl.multiple_of(target * own_rows, own_rows), own_rows)]
            send(chunk, normed_in.at[member], normed_sem.at[j], (base + target, core))
            send(pieces, partial_in.at[0, j], partial_sem.at[0, j], (base + target, core))
        send(pieces, partial_in.at[1, j], partial_sem.at[1, j], (base + target, 1 - core))
    normed_in[member] = normed[pl.ds(pl.multiple_of(member * own_rows, own_rows), own_rows), :]
    penalty = partial[pl.ds(member * per_member, per_member)]
    for j in range(PLANE):
        if j:
            arrived(normed_in.at[members[j]], normed_sem.at[j])
            arrived(partial_in.at[0, j], partial_sem.at[0, j])
            penalty = penalty + partial_in[0, j]
        arrived(partial_in.at[1, j], partial_sem.at[1, j])
        penalty = penalty + partial_in[1, j]
    penalty = penalty * (1.0 / (channels * PLANE * lax.axis_size("tp")) ** 0.5)
    for i in range(per_member):
        turned = jnp.broadcast_to(penalty[i][0:1, :], (GROUP, GROUP)).T
        turned = jnp.concatenate([turned] * (channels // GROUP), 1)
        span = pl.ds(i * GROUP, GROUP)
        for j in range(PLANE):
            value = normed_in[j, span, :].astype(F32) - turned * steer[:, j * channels : (j + 1) * channels]
            out_ref[span, j * channels : (j + 1) * channels] = value.astype(BF16)
    for copy, when in started:
        if when is None:
            copy.wait_send()
        else:
            pl.when(when)(lambda copy=copy: copy.wait_send())


def per_device(tokens, x_weight, bc_weight, dt_weight, conv_x, conv_bc, dt_bias, decay_rate, d_skip, norm_gain, initial_state, steer):
    planes = lax.axis_size("seq") // PLANE
    own_rows, columns = tokens.shape
    depth, all_channels = x_weight.shape
    all_heads = dt_weight.shape[1]
    channels, heads = all_channels // PLANE, all_heads // PLANE
    rows = own_rows * PLANE
    blocks = rows // GROUP
    quarter = bc_weight.shape[1] // PLANE

    vmem = pl.BlockSpec(memory_space=pltpu.VMEM)
    far = pl.BlockSpec(memory_space=pltpu.HBM)
    dma = pltpu.SemaphoreType.DMA
    out = pl.pallas_call(
        functools.partial(layer_kernel, planes, heads),
        out_shape=jax.ShapeDtypeStruct((own_rows, all_channels), BF16),
        in_specs=[far] * 12,
        out_specs=vmem,
        scratch_shapes=[
            pltpu.VMEM(bc_weight.shape, BF16),
            pltpu.VMEM((all_heads, depth), BF16),
            pltpu.VMEM((PLANE, quarter + TAIL, depth), BF16),
            pltpu.VMEM(conv_x.shape, F32),
            pltpu.VMEM(conv_bc.shape, F32),
            pltpu.VMEM((3, 1, all_heads), F32),
            pltpu.VMEM((8, 128), F32),
            pltpu.VMEM((1, all_channels), F32),
            pltpu.VMEM((channels, N), F32),
            pltpu.VMEM((1, all_channels), F32),
            dma((10,)),
            pltpu.VMEM((2, rows, columns), BF16),
            pltpu.VMEM((planes, PLANE, depth + quarter + TAIL, channels), BF16),
            pltpu.VMEM((planes * PLANE, depth, 128), BF16),
            pltpu.VMEM((rows, channels), F32),
            pltpu.VMEM((rows, 128), F32),
            pltpu.VMEM((TAIL, channels), BF16),
            pltpu.VMEM((TAIL, channels), BF16),
            pltpu.VMEM((quarter, rows), BF16),
            pltpu.VMEM((2 * PLANE, quarter, rows), BF16),
            pltpu.VMEM((2 * PLANE, quarter, GROUP), BF16),
            pltpu.VMEM((rows + TAIL, channels), F32),
            pltpu.VMEM((rows + TAIL, 2 * N), F32),
            pltpu.VMEM((rows, channels), BF16),
            pltpu.VMEM((rows, 2 * N), BF16),
            pltpu.VMEM((rows, 128), F32),
            pltpu.VMEM((rows, 128), F32),
            pltpu.VMEM((blocks, N, channels), F32),
            pltpu.VMEM((blocks, 8, 128), F32),
            pltpu.VMEM((rows, channels), F32),
            pltpu.VMEM((N, channels), BF16),
            pltpu.VMEM((8, 128), F32),
            pltpu.VMEM((planes, N, channels), BF16),
            pltpu.VMEM((planes, 8, 128), F32),
            pltpu.VMEM((rows, channels), BF16),
            pltpu.VMEM((blocks, 8, GROUP), F32),
            pltpu.VMEM((PLANE, own_rows, channels), BF16),
            pltpu.VMEM((2, PLANE, blocks // PLANE, 8, GROUP), F32),
            dma((64 + 10 * planes,)),
            dma((6,)),
            dma((PLANE, 2)),
            dma((PLANE,)),
            dma((2, planes, PLANE)),
            dma((3,)),
            dma(()),
            dma((2 * PLANE,)),
            dma((2 * PLANE,)),
            dma((planes,)),
            dma((planes,)),
            dma((PLANE,)),
            dma((2, PLANE)),
        ],
        compiler_params=pltpu.CompilerParams(collective_id=0, has_side_effects=True, vmem_limit_bytes=60 * 2**20),
    )(
        tokens, x_weight, bc_weight, dt_weight.T, conv_x, conv_bc, dt_bias[None, :], decay_rate[None, :], d_skip[None, :],
        norm_gain[None, :], initial_state.reshape(all_channels, N), steer[None, :],
    )
    return out


def solution(mesh):
    placed = (
        P("seq", "tp"),
        P("seq", "tp"),
        P("seq", "tp"),
        P("seq", "tp"),
        P(None, "tp"),
        P(),
        P("tp"),
        P("tp"),
        P("tp"),
        P("tp"),
        P("tp", None, None),
        P("tp"),
    )
    planar = mesh.shape["tp"] == 2 and mesh.shape["seq"] % PLANE == 0
    return jax.shard_map(
        per_device if planar else portable, mesh=mesh, in_specs=placed, out_specs=P("seq", "tp"), check_vma=False
    )
```
